32 devices in a mesh: section: 2 (over x), seq: 4 (over z), tp: 4 (over y, core).
Axes of the slice: x: 2, y: 2, z: 4, core: 2. Of those that a mesh axis runs over, the one named last changes fastest.
Arguments:
- layer_input: bfloat16 [2, 1024, 8192], P('section', 'seq', 'tp'), may hold values from -200 to 200, as said below
- norm_gain: float32 [2, 8192], P('section', 'tp'), may hold values from 0.1 to 1.9
- kv_cotangent: bfloat16 [2, 1024, 2048], P('section', 'seq', 'tp'), may hold values from -8 to 8
- kv_weight: bfloat16 [2, 2048, 8192], P('section', 'tp', 'seq'), may hold values from -0.09375 to 0.09375
- mlp_grads: bfloat16 [2, 1024, 8192], P('section', 'seq', 'tp'), may hold values from -6 to 6
- output_cotangent: bfloat16 [1024, 8192], P('seq', 'tp'), may hold values from -6 to 6
- out_weight: bfloat16 [2, 8192, 8192], P('section', 'tp', 'seq'), may hold values from -0.0625 to 0.0625
Outputs:
- attn_grads: bfloat16 [2, 1024, 8192], P('section', 'seq', 'tp')
- input_grads: bfloat16 [2, 1024, 8192], P('section', 'seq', 'tp')
The draws below stay inside these ranges and needn't reach their ends.
Inputs may be any that keep to these rules, and one draw needn't show every extreme that they name: `layer_input`: real-valued activations.
All inputs are finite; a program needn't handle non-finite values.
Results may differ from the reference program's by a relative error of at most 0.0055.
Values may be sent and summed in bfloat16 or wider, within the bound.
No kernel may reach another device: no remote copies, remote signals or barrier semaphores. Data moves between devices by JAX's collectives and lax.ppermute only.
A program may use at most 128 MiB of HBM per device.

```python
import math
import jax
import jax.numpy as jnp
from jax import lax

D = 8192
HH = 8192
KVW = 2048
TOKENS = 1024


def draw_layer_input(key, part):
    key = jax.random.fold_in(key, 17)
    key_base, key_row, key_col = jax.random.split(key, 3)
    position = jnp.arange(D, dtype=jnp.float32) / D
    col_scale = jnp.exp(jax.random.uniform(key_col, (2, 1, D), jnp.float32) * math.log(10.0))
    row_scale = jnp.exp(jax.random.uniform(key_row, (2, TOKENS, 1), jnp.float32) * math.log(10.0))
    base = jax.random.truncated_normal(key_base, -4.0, 4.0, (2, TOKENS, D), jnp.float32)
    rise = jnp.exp(position * 0.5 * math.log(3.0))
    return (0.1 * row_scale * col_scale * rise * base).astype(jnp.bfloat16)


def spiked(result, stream_key, source, target, shards_of, factor):
    def block_of(axis_at):
        return (jnp.arange(result.shape[axis_at]) // (result.shape[axis_at] // shards_of)).reshape((-1,) + (1,) * (result.ndim - 1 - axis_at))

    near = jax.random.permutation(stream_key, shards_of)[block_of(target)]
    second = (block_of(target) + shards_of // 2) % shards_of
    return jnp.where((block_of(source) == near) | (block_of(source) == second), factor * result, result)


def level_of(stream_key, dims, cuts, low, high):
    factor_of, own = 1.0, jax.random.fold_in(stream_key, 6)
    for dim, blocks in cuts:
        heights = jnp.exp(jax.random.uniform(jax.random.fold_in(own, dim), (blocks,), jnp.float32, low / len(cuts), high / len(cuts)))
        factor_of = factor_of * jnp.repeat(heights, dims[dim] // blocks).reshape([-1 if axis == dim else 1 for axis in range(len(dims))])
    return factor_of


def centred(key, dims, scale, bound, pieces=(), kind=jnp.bfloat16):
    values = jax.random.normal(key, dims, jnp.float32) * scale
    if len(pieces) > 0:
        values = level_of(key, dims, pieces, -0.22, 0.18) * values
    return jnp.clip(values, min=-bound, max=bound).astype(kind)


def noise_with(rng, extent, width, limit, pieces, heavy, held_as=jnp.bfloat16):
    array = width * jax.random.normal(rng, extent, jnp.float32)
    if pieces:
        array = array * level_of(rng, extent, pieces, -0.22, 0.18)
    return jnp.clip(spiked(array, jax.random.fold_in(rng, 3), *heavy), -limit, limit).astype(held_as)


def setup_inputs(seed: int = 0) -> dict:
    keys = jax.random.split(jax.random.key(seed), 8)
    return {
        "layer_input": draw_layer_input(jax.random.fold_in(keys[7], 71), 0),
        "norm_gain": jnp.clip(1.0 + 0.18 * jax.random.normal(keys[1], (2, D), jnp.float32), 0.1, 1.9),
        "kv_cotangent": centred(keys[2], (2, TOKENS, KVW), 2.0, 8.0, ((0, 2), (1, 4), (2, 4))),
        "kv_weight": noise_with(keys[3], (2, KVW, D), D ** -0.5, 0.09375, ((0, 2), (1, 4), (2, 4)), (1, 2, 4, 2.0)),
        "mlp_grads": centred(keys[4], (2, TOKENS, D), 1.0, 6.0, ((0, 2), (1, 4), (2, 4))),
        "output_cotangent": centred(keys[5], (TOKENS, D), 1.0, 6.0, ((0, 4), (1, 4))),
        "out_weight": centred(keys[6], (2, HH, D), HH ** -0.5, 0.0625, ((0, 2), (1, 4), (2, 4))),
    }


epsilon = 1e-05

def norm_backward(layer_input, norm_gain, kv_cotangent, kv_weight, slot):
    kv_terms = jnp.dot(kv_cotangent[slot], kv_weight[slot], preferred_element_type=jnp.float32)
    values = layer_input[slot].astype(jnp.float32)
    inv_rms = lax.rsqrt(lax.optimization_barrier(jnp.sum(values * values, axis=1, keepdims=True)) / D + epsilon)
    intersection = lax.optimization_barrier(jnp.sum(norm_gain[slot] * kv_terms * values, axis=1, keepdims=True))
    return inv_rms * norm_gain[slot] * kv_terms - values * (inv_rms * inv_rms * inv_rms) * intersection / D

def reference(layer_input, norm_gain, kv_cotangent, kv_weight, mlp_grads, output_cotangent, out_weight):
    back_one = norm_backward(layer_input, norm_gain, kv_cotangent, kv_weight, 1)
    back_zero = norm_backward(layer_input, norm_gain, kv_cotangent, kv_weight, 0)
    grad_one = output_cotangent.astype(jnp.float32) + mlp_grads[1].astype(jnp.float32)
    input_one = (grad_one + back_one).astype(jnp.bfloat16)
    grad_zero = input_one.astype(jnp.float32) + mlp_grads[0].astype(jnp.float32)
    input_zero = (grad_zero + back_zero).astype(jnp.bfloat16)
    attn_zero = jnp.dot(grad_zero.astype(jnp.bfloat16), out_weight[0].T, preferred_element_type=jnp.float32)
    attn_one = jnp.dot(grad_one.astype(jnp.bfloat16), out_weight[1].T, preferred_element_type=jnp.float32)
    attn_grads = jnp.stack([attn_zero, attn_one]).astype(jnp.bfloat16)
    input_grads = jnp.stack([input_zero, input_one])
    return (attn_grads, input_grads)
```

```python
import jax
import jax.numpy as jnp
from jax import lax
from jax.experimental import pallas as pl
from jax.experimental.pallas import tpu as pltpu
from jax.sharding import PartitionSpec as P

D = 8192


epsilon = 1e-05
CORES = 2
CHUNKS = 2


def from_behind(block, axis, distance):
    devices = range(lax.axis_size(axis))
    route = [(i - distance, i) for i in devices if i - distance in devices]
    return lax.ppermute(block, axis, route)


def sizes():
    seq, tp = lax.axis_size("seq"), lax.axis_size("tp")
    assert seq % tp == 0 and tp % CORES == 0
    return seq, tp, seq // tp


def over_rows(block, turn):
    tp = lax.axis_size("tp")
    return lax.ppermute(block, "tp", [(t, (t + turn * CORES) % tp) for t in range(tp)])


def over_cores(block):
    tp = lax.axis_size("tp")
    return lax.ppermute(block, "tp", [(t, t ^ 1) for t in range(tp)])


def exchange(block, axis):
    return lax.all_to_all(block, axis, 0, 0)


def to_slabs(block):
    seq, tp, ratio = sizes()
    tokens, width = block.shape
    parts = exchange(block.reshape(tp, tokens // tp, width), "tp")
    if ratio > 1:
        parts = parts.reshape(tp, tokens // tp, ratio, width // ratio).transpose(0, 2, 1, 3)
    return exchange(parts.reshape(seq, tokens // tp, width // ratio), "seq")


def from_slabs(block):
    seq, tp, ratio = sizes()
    _, tokens, width = block.shape
    parts = exchange(block, "seq")
    if ratio > 1:
        parts = parts.reshape(tp, ratio, tokens, width).transpose(0, 2, 1, 3)
    return exchange(parts.reshape(tp, tokens, width * ratio), "tp")


def gain_slab(gain):
    seq, tp, ratio = sizes()
    place, lane = lax.axis_index("seq"), lax.axis_index("tp")
    width = gain.shape[1] // ratio
    own = lax.dynamic_slice_in_dim(gain, place % ratio * width, width, 1)
    route = []
    for q in range(seq):
        for t in range(tp):
            to = (t * ratio + q % ratio, q // ratio)
            if to != (q, t):
                route.append((q * tp + t, to[0] * tp + to[1]))
    moved = lax.ppermute(own, ("seq", "tp"), route)
    stays = (place == lane * ratio + place % ratio) & (lane == place // ratio)
    return jnp.where(stays, own, moved)


def gather_seq(block):
    seq = lax.axis_size("seq")
    place = lax.axis_index("seq")
    arrived = [block]
    for turn in range(1, seq):
        route = [(q, (q + turn) % seq) for q in range(seq)]
        arrived.append(lax.ppermute(block, "seq", route))
    return jnp.stack([lax.select_n((place - q) % seq, *arrived) for q in range(seq)], axis=0)


def norm_backward(values, gain, kv_share, axes):
    squares, intersection = lax.psum(
        (jnp.sum(values * values, axis=-1), jnp.sum(gain * kv_share * values, axis=-1)), axes
    )
    inv_rms = lax.rsqrt(squares / D + epsilon)[..., None]
    return (
        inv_rms * gain * kv_share
        - values * (inv_rms * inv_rms * inv_rms) * intersection[..., None] / D
    )


def product_kernel(*refs):
    *pieces, weight, out, rows = refs
    seq, depth, width = pieces[0].shape

    @pl.when(pl.program_id(0) == 0)
    def _():
        for i, piece in enumerate(pieces):
            rows[i] = piece[...]

    terms = lax.dot_general(
        rows[...].reshape(-1, width),
        weight[...],
        (((1,), (1,)), ((), ())),
        preferred_element_type=jnp.float32,
    )
    for i in range(len(pieces)):
        for q in range(seq):
            start = (i * seq + q) * depth
            out[q, i] = terms[start : start + depth]


def product(pieces, weight):
    seq, depth, width = pieces[0].shape
    heads = weight.shape[0]
    block = min(512, heads)
    n = len(pieces)
    return pl.pallas_call(
        product_kernel,
        out_shape=jax.ShapeDtypeStruct((seq, n, depth, heads), jnp.float32),
        grid=(heads // block,),
        in_specs=[pl.BlockSpec((seq, depth, width), lambda i: (0, 0, 0)) for _ in pieces]
        + [pl.BlockSpec((block, width), lambda i: (i, 0))],
        out_specs=pl.BlockSpec((seq, n, depth, block), lambda i: (0, 0, 0, i)),
        scratch_shapes=[pltpu.VMEM((n, seq, depth, width), pieces[0].dtype)],
        compiler_params=pltpu.CompilerParams(
            dimension_semantics=("arbitrary",), vmem_limit_bytes=40 * 1024 * 1024
        ),
    )(*pieces, weight)


def body(layer_input, norm_gain, kv_cotangent, kv_weight, mlp_grads, output_cotangent, out_weight):
    seq, tp, ratio = sizes()
    row = tp // CORES
    upstream = lax.axis_index("section") == 0
    place, lane = lax.axis_index("seq"), lax.axis_index("tp")
    here, core = lane // CORES, lane % CORES
    tokens = kv_cotangent.shape[1]

    mixed = kv_cotangent[0].reshape(row, CORES, tokens // tp, -1)
    kept = lax.dynamic_index_in_dim(mixed, core, 1, keepdims=False)
    given = lax.dynamic_index_in_dim(mixed, 1 - core, 1, keepdims=False)
    cotangent = gather_seq(jnp.concatenate([kept, over_cores(given)], axis=2))
    weights = jnp.concatenate([kv_weight[0], over_cores(kv_weight[0])], axis=0)

    values = to_slabs(layer_input[0])
    branch = mlp_grads[0].astype(jnp.float32)
    grad_one = output_cotangent.astype(jnp.float32) + branch
    base_home = jnp.where(upstream, mlp_grads[0], grad_one.astype(jnp.bfloat16))
    base = to_slabs(base_home)
    gain = gain_slab(norm_gain)
    width = gain.shape[1]

    def kv_of(turn):
        part = lax.dynamic_index_in_dim(cotangent, (here + turn) % row, 1, keepdims=False)
        terms = jnp.dot(
            part.reshape(-1, part.shape[-1]), weights, preferred_element_type=jnp.float32
        )
        return terms.reshape(seq, tokens // tp, width)

    given = [over_rows(kv_of(turn).astype(jnp.bfloat16), turn) for turn in range(1, row)]
    kv_share = kv_of(0)
    for terms in given:
        kv_share = kv_share + terms.astype(jnp.float32)

    norm_back = norm_backward(values.astype(jnp.float32), gain, kv_share, "seq")
    input_one = (base.astype(jnp.float32) + norm_back).astype(jnp.bfloat16)

    depth = tokens // tp // CHUNKS

    def cut(array, c):
        return array[:, c * depth : (c + 1) * depth]

    arrivals = [from_behind(cut(input_one, c), "section", -1) for c in range(CHUNKS)]
    home = from_slabs(norm_back.astype(jnp.bfloat16))
    blocks_of = []
    for c in range(CHUNKS):
        part = cut(base, c)
        arriving = arrivals[c]
        if c > 0:
            arriving, blocks[-1] = lax.optimization_barrier((arriving, blocks[-1]))
        grad_zero = arriving.astype(jnp.float32) + part.astype(jnp.float32)
        grad = jnp.where(upstream, grad_zero.astype(jnp.bfloat16), part)
        blocks = [over_rows(grad, turn) if turn else grad for turn in range(row)]
        blocks_of.append(blocks)
    attn_parts = []
    for c, blocks in enumerate(blocks_of):
        pieces = [half for block in blocks for half in (block, over_cores(block))]
        terms = product(pieces, out_weight[0])
        total = None
        for step in range(1, seq + 1):
            mine = lax.dynamic_index_in_dim(terms, (place - step) % seq, 0, keepdims=False)
            if total is not None:
                mine = mine + total.astype(jnp.float32)
            mine = mine.astype(jnp.bfloat16)
            if step < seq:
                total = lax.ppermute(mine, "seq", [(q, (q + 1) % seq) for q in range(seq)])
        attn_parts.append(mine)
    attn_part = jnp.concatenate(attn_parts, axis=1)
    order = []
    for t in range(tp):
        which = (here - t // CORES) % row * CORES + (lane + t) % CORES
        order.append(lax.dynamic_index_in_dim(attn_part, which, 0, keepdims=False))
    attn_part = jnp.concatenate(order, axis=0)

    home = home.reshape(tokens, -1).astype(jnp.float32)
    own = (grad_one + home).astype(jnp.bfloat16)
    arrived = from_behind(own, "section", -1)
    input_zero = (arrived.astype(jnp.float32) + branch + home).astype(jnp.bfloat16)
    input_part = jnp.where(upstream, input_zero, own)
    return (attn_part[None], input_part[None])


def solution(mesh):
    in_specs = (
        P("section", "seq", "tp"),
        P("section", "tp"),
        P("section", "seq", "tp"),
        P("section", "tp", "seq"),
        P("section", "seq", "tp"),
        P("seq", "tp"),
        P("section", "tp", "seq"),
    )
    out_specs = (P("section", "seq", "tp"), P("section", "seq", "tp"))
    return jax.shard_map(body, mesh=mesh, in_specs=in_specs, out_specs=out_specs, check_vma=False)
```

```python
import jax
import jax.numpy as jnp
from jax import lax
from jax.experimental import pallas as pl
from jax.experimental.pallas import tpu as pltpu
from jax.sharding import PartitionSpec as P

D = 8192


epsilon = 1e-05
CORES = 2
CHUNKS = 2


def from_behind(block, axis, distance):
    devices = range(lax.axis_size(axis))
    route = [(i - distance, i) for i in devices if i - distance in devices]
    return lax.ppermute(block, axis, route)


def after(value, *others):
    return lax.optimization_barrier((value, *others))[0]


def sizes():
    seq, tp = lax.axis_size("seq"), lax.axis_size("tp")
    assert seq % tp == 0 and tp % CORES == 0
    return seq, tp, seq // tp


def over_rows(block, turn):
    tp = lax.axis_size("tp")
    return lax.ppermute(block, "tp", [(t, (t + turn * CORES) % tp) for t in range(tp)])


def over_cores(block):
    tp = lax.axis_size("tp")
    return lax.ppermute(block, "tp", [(t, t ^ 1) for t in range(tp)])


def exchange(block, axis):
    return lax.all_to_all(block, axis, 0, 0)


def mix_tokens(blocks):
    tp = lax.axis_size("tp")
    tokens, width = blocks[0].shape
    stacked = jnp.stack([block.reshape(tp, tokens // tp, width) for block in blocks], axis=1)
    return exchange(stacked, "tp")


def to_slabs(parts):
    seq, tp, ratio = sizes()
    _, count, tokens, width = parts.shape
    if ratio > 1:
        parts = parts.reshape(tp, count, tokens, ratio, width // ratio).transpose(0, 3, 1, 2, 4)
    return exchange(parts.reshape(seq, count, tokens, width // ratio), "seq")


def slabs_by_permutes(blocks):
    seq, tp, _ = sizes()
    place, lane = lax.axis_index("seq"), lax.axis_index("tp")
    here, core = lane // CORES, lane % CORES
    tokens, width = blocks[0].shape
    stacked = jnp.stack(
        [block.reshape(tp // CORES, CORES, tokens // tp, width) for block in blocks], axis=2
    )
    near = lax.dynamic_index_in_dim(stacked, here, 0, keepdims=False)
    far = over_rows(lax.dynamic_index_in_dim(stacked, 1 - here, 0, keepdims=False), 1)
    return near, far


def spread(near, far):
    seq, tp, _ = sizes()
    place, lane = lax.axis_index("seq"), lax.axis_index("tp")
    here, core = lane // CORES, lane % CORES
    arrived = []
    for j in range(seq):
        slot = place ^ j
        piece = jnp.where(
            slot // CORES == here,
            lax.dynamic_index_in_dim(near, slot % CORES, 0, keepdims=False),
            lax.dynamic_index_in_dim(far, slot % CORES, 0, keepdims=False),
        )
        route = []
        for q in range(seq):
            for t in range(tp):
                to = (t % CORES + (q ^ j) // CORES * CORES, t // CORES * CORES + (q ^ j) % CORES)
                if to != (q, t):
                    route.append((q * tp + t, to[0] * tp + to[1]))
        moved = lax.ppermute(piece, ("seq", "tp"), route)
        if j == 0:
            moved = jnp.where(core == place % CORES, piece, moved)
        arrived.append(moved)
    slot = place // CORES * CORES + core
    return jnp.stack([lax.select_n(slot ^ q, *arrived) for q in range(seq)], axis=0)


def mix_features(block):
    seq, tp, ratio = sizes()
    _, tokens, width = block.shape
    parts = exchange(block, "seq")
    if ratio > 1:
        parts = parts.reshape(tp, ratio, tokens, width).transpose(0, 2, 1, 3)
    return parts.reshape(tp, tokens, width * ratio)


def gain_slab(gain):
    seq, tp, ratio = sizes()
    place, lane = lax.axis_index("seq"), lax.axis_index("tp")
    width = gain.shape[1] // ratio
    own = lax.dynamic_slice_in_dim(gain, place % ratio * width, width, 1)
    route = []
    for q in range(seq):
        for t in range(tp):
            to = (t * ratio + q % ratio, q // ratio)
            if to != (q, t):
                route.append((q * tp + t, to[0] * tp + to[1]))
    moved = lax.ppermute(own, ("seq", "tp"), route)
    stays = (place == lane * ratio + place % ratio) & (lane == place // ratio)
    return jnp.where(stays, own, moved)


def gather_seq(block):
    seq = lax.axis_size("seq")
    place = lax.axis_index("seq")
    arrived = [block]
    for turn in range(1, seq):
        route = [(q, (q + turn) % seq) for q in range(seq)]
        arrived.append(lax.ppermute(block, "seq", route))
    return jnp.stack([lax.select_n((place - q) % seq, *arrived) for q in range(seq)], axis=0)


def norm_backward(values, gain, kv_share, axes):
    squares, intersection = lax.psum(
        (jnp.sum(values * values, axis=-1), jnp.sum(gain * kv_share * values, axis=-1)), axes
    )
    inv_rms = lax.rsqrt(squares / D + epsilon)[..., None]
    return (
        inv_rms * gain * kv_share
        - values * (inv_rms * inv_rms * inv_rms) * intersection[..., None] / D
    )


def product_kernel(*refs):
    *pieces, weight, out, rows, blocks, sems = refs
    seq, depth, width = pieces[0].shape
    count, block, _ = blocks.shape

    def copy(b):
        part = weight.at[pl.ds(b * block, block)]
        return pltpu.make_async_copy(part, blocks.at[b], sems.at[b])

    for b in range(count):
        copy(b).start()
    for i, piece in enumerate(pieces):
        rows[i] = piece[...]
    for b in range(count):
        copy(b).wait()
        terms = lax.dot_general(
            rows[...].reshape(-1, width),
            blocks[b],
            (((1,), (1,)), ((), ())),
            preferred_element_type=jnp.float32,
        ).astype(out.dtype)
        for i in range(len(pieces)):
            for q in range(seq):
                start = (i * seq + q) * depth
                out[q, i, :, b * block : (b + 1) * block] = terms[start : start + depth]


def product(pieces, weight):
    seq, depth, width = pieces[0].shape
    heads = weight.shape[0]
    block = min(512, heads)
    n = len(pieces)
    return pl.pallas_call(
        product_kernel,
        out_shape=jax.ShapeDtypeStruct((seq, n, depth, heads), jnp.bfloat16),
        in_specs=[pl.BlockSpec(memory_space=pltpu.VMEM) for _ in pieces]
        + [pl.BlockSpec(memory_space=pltpu.HBM)],
        out_specs=pl.BlockSpec(memory_space=pltpu.VMEM),
        cost_estimate=pl.CostEstimate(
            flops=2 * n * seq * depth * width * heads,
            bytes_accessed=2 * heads * width + 2 * n * seq * depth * (heads + width),
            transcendentals=0,
        ),
        scratch_shapes=[
            pltpu.VMEM((n, seq, depth, width), pieces[0].dtype),
            pltpu.VMEM((heads // block, block, width), weight.dtype),
            pltpu.SemaphoreType.DMA((heads // block,)),
        ],
        compiler_params=pltpu.CompilerParams(vmem_limit_bytes=24 * 1024 * 1024),
    )(*pieces, weight)


def body(layer_input, norm_gain, kv_cotangent, kv_weight, mlp_grads, output_cotangent, out_weight):
    seq, tp, ratio = sizes()
    row = tp // CORES
    upstream = lax.axis_index("section") == 0
    place, lane = lax.axis_index("seq"), lax.axis_index("tp")
    here, core = lane // CORES, lane % CORES
    tokens = kv_cotangent.shape[1]

    mixed = kv_cotangent[0].reshape(row, CORES, tokens // tp, -1)
    kept = lax.dynamic_index_in_dim(mixed, core, 1, keepdims=False)
    given = lax.dynamic_index_in_dim(mixed, 1 - core, 1, keepdims=False)
    given = over_cores(given)
    cotangent = gather_seq(jnp.concatenate([kept, given], axis=2))
    weights = jnp.concatenate([kv_weight[0], over_cores(kv_weight[0])], axis=0)

    branch = mlp_grads[0].astype(jnp.float32)
    grad_one = output_cotangent.astype(jnp.float32) + branch
    base_home = jnp.where(upstream, mlp_grads[0], grad_one.astype(jnp.bfloat16))
    gain = gain_slab(norm_gain)
    width = gain.shape[1]

    def kv_of(turn):
        part = lax.dynamic_index_in_dim(cotangent, (here + turn) % row, 1, keepdims=False)
        terms = jnp.dot(
            part.reshape(-1, part.shape[-1]), weights, preferred_element_type=jnp.float32
        )
        return terms.reshape(seq, tokens // tp, width)

    given = [kv_of(turn).astype(jnp.bfloat16) for turn in range(1, row)]
    blocks = [layer_input[0], base_home]
    if seq == tp == 2 * CORES:
        near, far = slabs_by_permutes(blocks)
        far = after(far, *given)
        slabs = spread(near, far)
    else:
        slabs = to_slabs(mix_tokens(blocks))
    given = [over_rows(terms, turn) for turn, terms in enumerate(given, 1)]
    kv_share, slabs = lax.optimization_barrier((kv_of(0), slabs))
    values, base = slabs[:, 0], slabs[:, 1]
    for terms in given:
        kv_share = kv_share + terms.astype(jnp.float32)

    norm_back = norm_backward(values.astype(jnp.float32), gain, kv_share, "seq")
    input_one = (base.astype(jnp.float32) + norm_back).astype(jnp.bfloat16)

    depth = tokens // tp // CHUNKS

    def cut(array, c):
        return array[:, c * depth : (c + 1) * depth]

    arrivals = [from_behind(cut(input_one, c), "section", -1) for c in range(CHUNKS)]
    home = mix_features(norm_back.astype(jnp.bfloat16))
    blocks_of = []
    for c in range(CHUNKS):
        part = cut(base, c)
        arriving = arrivals[c]
        if c > 0:
            arriving = after(arriving, blocks[-1])
        grad_zero = arriving.astype(jnp.float32) + part.astype(jnp.float32)
        grad = jnp.where(upstream, grad_zero.astype(jnp.bfloat16), part)
        blocks = [over_rows(grad, turn) if turn else grad for turn in range(row)]
        blocks_of.append(blocks)
    attn_parts = []
    for c, blocks in enumerate(blocks_of):
        if c == 0:
            blocks[-1] = after(blocks[-1], home)
        else:
            blocks[-1] = after(blocks[-1], attn_parts[-1][0])
        pieces = [half for block in blocks for half in (block, over_cores(block))]
        terms = product(pieces, out_weight[0])
        first = lax.dynamic_index_in_dim(terms, (place - 1) % seq, 0, keepdims=False)
        attn_parts.append([first, terms])
    home = after(home, attn_parts[-1][0])
    for c, (mine, terms) in enumerate(attn_parts):
        for step in range(2, seq + 1):
            total = lax.ppermute(mine, "seq", [(q, (q + 1) % seq) for q in range(seq)])
            mine = lax.dynamic_index_in_dim(terms, (place - step) % seq, 0, keepdims=False)
            mine = mine.astype(jnp.float32) + total.astype(jnp.float32)
            mine = mine.astype(jnp.bfloat16)
        attn_parts[c] = mine
    attn_part = jnp.concatenate(attn_parts, axis=1)
    order = []
    for t in range(tp):
        which = (here - t // CORES) % row * CORES + (lane + t) % CORES
        order.append(lax.dynamic_index_in_dim(attn_part, which, 0, keepdims=False))
    attn_part = jnp.concatenate(order, axis=0)

    home = exchange(home, "tp").reshape(tokens, -1).astype(jnp.float32)
    own = (grad_one + home).astype(jnp.bfloat16)
    arrived = from_behind(own, "section", -1)
    input_zero = (arrived.astype(jnp.float32) + branch + home).astype(jnp.bfloat16)
    input_part = jnp.where(upstream, input_zero, own)
    return (attn_part[None], input_part[None])


def solution(mesh):
    in_specs = (
        P("section", "seq", "tp"),
        P("section", "tp"),
        P("section", "seq", "tp"),
        P("section", "tp", "seq"),
        P("section", "seq", "tp"),
        P("seq", "tp"),
        P("section", "tp", "seq"),
    )
    out_specs = (P("section", "seq", "tp"), P("section", "seq", "tp"))
    return jax.shard_map(body, mesh=mesh, in_specs=in_specs, out_specs=out_specs, check_vma=False)
```

```python
import jax
import jax.numpy as jnp
from jax import lax
from jax.experimental import pallas as pl
from jax.experimental.pallas import tpu as pltpu
from jax.sharding import PartitionSpec as P

D = 8192


epsilon = 1e-05
CORES = 2
CHUNKS = 2


def from_behind(block, axis, distance):
    devices = range(lax.axis_size(axis))
    route = [(i - distance, i) for i in devices if i - distance in devices]
    return lax.ppermute(block, axis, route)


def after(value, *others):
    return lax.optimization_barrier((value, *others))[0]


def sizes():
    seq, tp = lax.axis_size("seq"), lax.axis_size("tp")
    assert seq % tp == 0 and tp % CORES == 0
    return seq, tp, seq // tp


def over_rows(block, turn):
    tp = lax.axis_size("tp")
    return lax.ppermute(block, "tp", [(t, (t + turn * CORES) % tp) for t in range(tp)])


def over_cores(block):
    tp = lax.axis_size("tp")
    return lax.ppermute(block, "tp", [(t, t ^ 1) for t in range(tp)])


def exchange(block, axis):
    return lax.all_to_all(block, axis, 0, 0)


def mix_tokens(blocks):
    tp = lax.axis_size("tp")
    tokens, width = blocks[0].shape
    stacked = jnp.stack([block.reshape(tp, tokens // tp, width) for block in blocks], axis=1)
    return exchange(stacked, "tp")


def to_slabs(parts):
    seq, tp, ratio = sizes()
    _, count, tokens, width = parts.shape
    if ratio > 1:
        parts = parts.reshape(tp, count, tokens, ratio, width // ratio).transpose(0, 3, 1, 2, 4)
    return exchange(parts.reshape(seq, count, tokens, width // ratio), "seq")


def slabs_by_permutes(blocks):
    seq, tp, _ = sizes()
    place, lane = lax.axis_index("seq"), lax.axis_index("tp")
    here, core = lane // CORES, lane % CORES
    tokens, width = blocks[0].shape
    stacked = jnp.stack(
        [block.reshape(tp // CORES, CORES, tokens // tp, width) for block in blocks], axis=2
    )
    near = lax.dynamic_index_in_dim(stacked, here, 0, keepdims=False)
    far = over_rows(lax.dynamic_index_in_dim(stacked, 1 - here, 0, keepdims=False), 1)
    return near, far


def spread(near, far):
    seq, tp, _ = sizes()
    place, lane = lax.axis_index("seq"), lax.axis_index("tp")
    here, core = lane // CORES, lane % CORES
    arrived = []
    for j in range(seq):
        slot = place ^ j
        piece = jnp.where(
            slot // CORES == here,
            lax.dynamic_index_in_dim(near, slot % CORES, 0, keepdims=False),
            lax.dynamic_index_in_dim(far, slot % CORES, 0, keepdims=False),
        )
        route = []
        for q in range(seq):
            for t in range(tp):
                to = (t % CORES + (q ^ j) // CORES * CORES, t // CORES * CORES + (q ^ j) % CORES)
                if to != (q, t):
                    route.append((q * tp + t, to[0] * tp + to[1]))
        moved = lax.ppermute(piece, ("seq", "tp"), route)
        if j == 0:
            moved = jnp.where(core == place % CORES, piece, moved)
        arrived.append(moved)
    slot = place // CORES * CORES + core
    return jnp.stack([lax.select_n(slot ^ q, *arrived) for q in range(seq)], axis=0)


def mix_features(block):
    seq, tp, ratio = sizes()
    _, tokens, width = block.shape
    parts = exchange(block, "seq")
    if ratio > 1:
        parts = parts.reshape(tp, ratio, tokens, width).transpose(0, 2, 1, 3)
    return parts.reshape(tp, tokens, width * ratio)


def gain_slab(gain):
    seq, tp, ratio = sizes()
    place, lane = lax.axis_index("seq"), lax.axis_index("tp")
    width = gain.shape[1] // ratio
    own = lax.dynamic_slice_in_dim(gain, place % ratio * width, width, 1)
    route = []
    for q in range(seq):
        for t in range(tp):
            to = (t * ratio + q % ratio, q // ratio)
            if to != (q, t):
                route.append((q * tp + t, to[0] * tp + to[1]))
    moved = lax.ppermute(own, ("seq", "tp"), route)
    stays = (place == lane * ratio + place % ratio) & (lane == place // ratio)
    return jnp.where(stays, own, moved)


def gather_seq(block):
    seq = lax.axis_size("seq")
    place = lax.axis_index("seq")
    arrived = [block]
    for turn in range(1, seq):
        route = [(q, (q + turn) % seq) for q in range(seq)]
        arrived.append(lax.ppermute(block, "seq", route))
    return jnp.stack([lax.select_n((place - q) % seq, *arrived) for q in range(seq)], axis=0)


def norm_backward(values, gain, kv_share):
    sums = jnp.stack([jnp.sum(values * values, axis=-1), jnp.sum(gain * kv_share * values, axis=-1)])
    short = lax.axis_size("seq") <= 2 * CORES
    squares, intersection = jnp.sum(gather_seq(sums), axis=0) if short else lax.psum(sums, "seq")
    inv_rms = lax.rsqrt(squares / D + epsilon)[..., None]
    return (
        inv_rms * gain * kv_share
        - values * (inv_rms * inv_rms * inv_rms) * intersection[..., None] / D
    )


def product_kernel(*refs):
    *pieces, weight, out, rows = refs
    seq, depth, width = pieces[0].shape

    @pl.when(pl.program_id(0) == 0)
    def _():
        for i, piece in enumerate(pieces):
            rows[i] = piece[...]

    terms = lax.dot_general(
        rows[...].reshape(-1, width),
        weight[...],
        (((1,), (1,)), ((), ())),
        preferred_element_type=jnp.float32,
    ).astype(out.dtype)
    for i in range(len(pieces)):
        for q in range(seq):
            start = (i * seq + q) * depth
            out[q, i] = terms[start : start + depth]


def product(pieces, weight):
    seq, depth, width = pieces[0].shape
    heads = weight.shape[0]
    block = min(512, heads)
    n = len(pieces)
    return pl.pallas_call(
        product_kernel,
        out_shape=jax.ShapeDtypeStruct((seq, n, depth, heads), jnp.bfloat16),
        grid=(heads // block,),
        in_specs=[pl.BlockSpec((seq, depth, width), lambda i: (0, 0, 0)) for _ in pieces]
        + [pl.BlockSpec((block, width), lambda i: (i, 0))],
        out_specs=pl.BlockSpec((seq, n, depth, block), lambda i: (0, 0, 0, i)),
        cost_estimate=pl.CostEstimate(
            flops=2 * n * seq * depth * width * heads,
            bytes_accessed=2 * heads * width + 2 * n * seq * depth * heads,
            transcendentals=0,
        ),
        scratch_shapes=[pltpu.VMEM((n, seq, depth, width), pieces[0].dtype)],
        compiler_params=pltpu.CompilerParams(
            dimension_semantics=("arbitrary",), vmem_limit_bytes=44 * 1024 * 1024
        ),
    )(*pieces, weight)


def body(layer_input, norm_gain, kv_cotangent, kv_weight, mlp_grads, output_cotangent, out_weight):
    seq, tp, ratio = sizes()
    row = tp // CORES
    upstream = lax.axis_index("section") == 0
    place, lane = lax.axis_index("seq"), lax.axis_index("tp")
    here, core = lane // CORES, lane % CORES
    tokens = kv_cotangent.shape[1]

    mixed = kv_cotangent[0].reshape(row, CORES, tokens // tp, -1)
    kept = lax.dynamic_index_in_dim(mixed, core, 1, keepdims=False)
    given = lax.dynamic_index_in_dim(mixed, 1 - core, 1, keepdims=False)
    given = over_cores(given)
    cotangent = gather_seq(jnp.concatenate([kept, given], axis=2))
    weights = jnp.concatenate([kv_weight[0], over_cores(kv_weight[0])], axis=0)

    branch = mlp_grads[0].astype(jnp.float32)
    grad_one = output_cotangent.astype(jnp.float32) + branch
    base_home = jnp.where(upstream, mlp_grads[0], grad_one.astype(jnp.bfloat16))
    gain = gain_slab(norm_gain)
    width = gain.shape[1]

    def kv_of(turn):
        part = lax.dynamic_index_in_dim(cotangent, (here + turn) % row, 1, keepdims=False)
        terms = jnp.dot(
            part.reshape(-1, part.shape[-1]), weights, preferred_element_type=jnp.float32
        )
        return terms.reshape(seq, tokens // tp, width)

    given = [kv_of(turn).astype(jnp.bfloat16) for turn in range(1, row)]
    blocks = [layer_input[0], base_home]
    if seq == tp == 2 * CORES:
        near, far = slabs_by_permutes(blocks)
        far = after(far, *given)
        slabs = spread(near, far)
    else:
        slabs = to_slabs(mix_tokens(blocks))
    given = [over_rows(terms, turn) for turn, terms in enumerate(given, 1)]
    kv_share, slabs = lax.optimization_barrier((kv_of(0), slabs))
    values, base = slabs[:, 0], slabs[:, 1]
    for terms in given:
        kv_share = kv_share + terms.astype(jnp.float32)

    norm_back = norm_backward(values.astype(jnp.float32), gain, kv_share)
    input_one = (base.astype(jnp.float32) + norm_back).astype(jnp.bfloat16)

    depth = tokens // tp // CHUNKS

    def cut(array, c):
        return array[:, c * depth : (c + 1) * depth]

    leaving = [cut(input_one, c) for c in range(CHUNKS)]
    arrivals = [from_behind(part, "section", -1) for part in leaving]
    home = mix_features(after(norm_back.astype(jnp.bfloat16), leaving[-1]))
    blocks_of = []
    for c in range(CHUNKS):
        part = cut(base, c)
        arriving = arrivals[c]
        if c > 0:
            arriving = after(arriving, blocks[-1])
        grad_zero = arriving.astype(jnp.float32) + part.astype(jnp.float32)
        grad = jnp.where(upstream, grad_zero.astype(jnp.bfloat16), part)
        blocks = [over_rows(grad, turn) if turn else grad for turn in range(row)]
        blocks_of.append(blocks)
    attn_parts = []
    for c, blocks in enumerate(blocks_of):
        if c > 0:
            blocks[-1] = after(blocks[-1], attn_parts[-1][0])
        pieces = [half for block in blocks for half in (block, over_cores(block))]
        terms = product(pieces, out_weight[0])
        first = lax.dynamic_index_in_dim(terms, (place - 1) % seq, 0, keepdims=False)
        if c == 0:
            first = after(first, home)
        attn_parts.append([first, terms])
    home = exchange(after(home, attn_parts[-1][0]), "tp")
    home = home.reshape(tokens, -1).astype(jnp.float32)
    own = (grad_one + home).astype(jnp.bfloat16)
    arrived = from_behind(own, "section", -1)
    for c, (mine, terms) in enumerate(attn_parts):
        for step in range(2, seq + 1):
            total = lax.ppermute(mine, "seq", [(q, (q + 1) % seq) for q in range(seq)])
            if c == 0 and step == 3:
                total = after(total, own)
            if c == CHUNKS - 1 and step == seq:
                total = after(total, arrived)
            mine = lax.dynamic_index_in_dim(terms, (place - step) % seq, 0, keepdims=False)
            mine = mine.astype(jnp.float32) + total.astype(jnp.float32)
            mine = mine.astype(jnp.bfloat16)
        attn_parts[c] = mine
    attn_part = jnp.concatenate(attn_parts, axis=1)
    order = []
    for t in range(tp):
        which = (here - t // CORES) % row * CORES + (lane + t) % CORES
        order.append(lax.dynamic_index_in_dim(attn_part, which, 0, keepdims=False))
    attn_part = jnp.concatenate(order, axis=0)

    input_zero = (arrived.astype(jnp.float32) + branch + home).astype(jnp.bfloat16)
    input_part = jnp.where(upstream, input_zero, own)
    return (attn_part[None], input_part[None])


def solution(mesh):
    in_specs = (
        P("section", "seq", "tp"),
        P("section", "tp"),
        P("section", "seq", "tp"),
        P("section", "tp", "seq"),
        P("section", "seq", "tp"),
        P("seq", "tp"),
        P("section", "tp", "seq"),
    )
    out_specs = (P("section", "seq", "tp"), P("section", "seq", "tp"))
    return jax.shard_map(body, mesh=mesh, in_specs=in_specs, out_specs=out_specs, check_vma=False)
```

```python
import jax
import jax.numpy as jnp
from jax import lax
from jax.experimental import pallas as pl
from jax.experimental.pallas import tpu as pltpu
from jax.sharding import PartitionSpec as P

D = 8192


epsilon = 1e-05
CORES = 2
CHUNKS = 2


def from_behind(block, axis, distance):
    devices = range(lax.axis_size(axis))
    route = [(i - distance, i) for i in devices if i - distance in devices]
    return lax.ppermute(block, axis, route)


def after(value, *others):
    return lax.optimization_barrier((value, *others))[0]


def sizes():
    seq, tp = lax.axis_size("seq"), lax.axis_size("tp")
    assert seq % tp == 0 and tp % CORES == 0
    return seq, tp, seq // tp


def over_rows(block, turn):
    tp = lax.axis_size("tp")
    return lax.ppermute(block, "tp", [(t, (t + turn * CORES) % tp) for t in range(tp)])


def over_cores(block):
    tp = lax.axis_size("tp")
    return lax.ppermute(block, "tp", [(t, t ^ 1) for t in range(tp)])


def exchange(block, axis):
    return lax.all_to_all(block, axis, 0, 0)


def mix_tokens(blocks):
    tp = lax.axis_size("tp")
    tokens, width = blocks[0].shape
    stacked = jnp.stack([block.reshape(tp, tokens // tp, width) for block in blocks], axis=1)
    return exchange(stacked, "tp")


def to_slabs(parts):
    seq, tp, ratio = sizes()
    _, count, tokens, width = parts.shape
    if ratio > 1:
        parts = parts.reshape(tp, count, tokens, ratio, width // ratio).transpose(0, 3, 1, 2, 4)
    return exchange(parts.reshape(seq, count, tokens, width // ratio), "seq")


def slabs_by_permutes(blocks):
    seq, tp, _ = sizes()
    place, lane = lax.axis_index("seq"), lax.axis_index("tp")
    here, core = lane // CORES, lane % CORES
    tokens, width = blocks[0].shape
    stacked = jnp.stack(
        [block.reshape(tp // CORES, CORES, tokens // tp, width) for block in blocks], axis=2
    )
    near = lax.dynamic_index_in_dim(stacked, here, 0, keepdims=False)
    far = over_rows(lax.dynamic_index_in_dim(stacked, 1 - here, 0, keepdims=False), 1)
    return near, far


def spread(near, far):
    seq, tp, _ = sizes()
    place, lane = lax.axis_index("seq"), lax.axis_index("tp")
    here, core = lane // CORES, lane % CORES
    arrived = []
    for j in range(seq):
        slot = place ^ j
        piece = jnp.where(
            slot // CORES == here,
            lax.dynamic_index_in_dim(near, slot % CORES, 0, keepdims=False),
            lax.dynamic_index_in_dim(far, slot % CORES, 0, keepdims=False),
        )
        route = []
        for q in range(seq):
            for t in range(tp):
                to = (t % CORES + (q ^ j) // CORES * CORES, t // CORES * CORES + (q ^ j) % CORES)
                if to != (q, t):
                    route.append((q * tp + t, to[0] * tp + to[1]))
        moved = lax.ppermute(piece, ("seq", "tp"), route)
        if j == 0:
            moved = jnp.where(core == place % CORES, piece, moved)
        arrived.append(moved)
    return arrived, place // CORES * CORES + core


def collect(arrived, slot):
    return jnp.stack([lax.select_n(slot ^ q, *arrived) for q in range(len(arrived))], axis=0)


def mix_features(block):
    seq, tp, ratio = sizes()
    _, tokens, width = block.shape
    parts = exchange(block, "seq")
    if ratio > 1:
        parts = parts.reshape(tp, ratio, tokens, width).transpose(0, 2, 1, 3)
    return parts.reshape(tp, tokens, width * ratio)


def gain_slab(gain):
    seq, tp, ratio = sizes()
    place, lane = lax.axis_index("seq"), lax.axis_index("tp")
    width = gain.shape[1] // ratio
    own = lax.dynamic_slice_in_dim(gain, place % ratio * width, width, 1)
    route = []
    for q in range(seq):
        for t in range(tp):
            to = (t * ratio + q % ratio, q // ratio)
            if to != (q, t):
                route.append((q * tp + t, to[0] * tp + to[1]))
    moved = lax.ppermute(own, ("seq", "tp"), route)
    stays = (place == lane * ratio + place % ratio) & (lane == place // ratio)
    return jnp.where(stays, own, moved)


def gather_seq(block):
    seq = lax.axis_size("seq")
    arrived = [block]
    for turn in range(1, seq):
        route = [(q, (q + turn) % seq) for q in range(seq)]
        arrived.append(lax.ppermute(block, "seq", route))
    return arrived


def by_place(arrived):
    seq = len(arrived)
    place = lax.axis_index("seq")
    return jnp.stack([lax.select_n((place - q) % seq, *arrived) for q in range(seq)], axis=0)


def local_sums(values, gain, kv_share):
    return jnp.stack([jnp.sum(values * values, axis=-1), jnp.sum(gain * kv_share * values, axis=-1)])


def norm_backward(values, gain, kv_share, sums):
    short = lax.axis_size("seq") <= 2 * CORES
    squares, intersection = jnp.sum(by_place(gather_seq(sums)), axis=0) if short else lax.psum(sums, "seq")
    inv_rms = lax.rsqrt(squares / D + epsilon)[..., None]
    return (
        inv_rms * gain * kv_share
        - values * (inv_rms * inv_rms * inv_rms) * intersection[..., None] / D
    )


def product_kernel(*refs):
    *pieces, weight, out, rows = refs
    seq, depth, width = pieces[0].shape

    @pl.when(pl.program_id(0) == 0)
    def _():
        for i, piece in enumerate(pieces):
            rows[i] = piece[...]

    terms = lax.dot_general(
        rows[...].reshape(-1, width),
        weight[...],
        (((1,), (1,)), ((), ())),
        preferred_element_type=jnp.float32,
    ).astype(out.dtype)
    for i in range(len(pieces)):
        for q in range(seq):
            start = (i * seq + q) * depth
            out[q, i] = terms[start : start + depth]


def product(pieces, weight):
    seq, depth, width = pieces[0].shape
    heads = weight.shape[0]
    block = min(512, heads)
    n = len(pieces)
    return pl.pallas_call(
        product_kernel,
        out_shape=jax.ShapeDtypeStruct((seq, n, depth, heads), jnp.bfloat16),
        grid=(heads // block,),
        in_specs=[pl.BlockSpec((seq, depth, width), lambda i: (0, 0, 0)) for _ in pieces]
        + [pl.BlockSpec((block, width), lambda i: (i, 0))],
        out_specs=pl.BlockSpec((seq, n, depth, block), lambda i: (0, 0, 0, i)),
        cost_estimate=pl.CostEstimate(
            flops=2 * n * seq * depth * width * heads,
            bytes_accessed=2 * heads * width + 2 * n * seq * depth * heads,
            transcendentals=0,
        ),
        scratch_shapes=[pltpu.VMEM((n, seq, depth, width), pieces[0].dtype)],
        compiler_params=pltpu.CompilerParams(
            dimension_semantics=("arbitrary",), vmem_limit_bytes=44 * 1024 * 1024
        ),
    )(*pieces, weight)


def body(layer_input, norm_gain, kv_cotangent, kv_weight, mlp_grads, output_cotangent, out_weight):
    seq, tp, ratio = sizes()
    row = tp // CORES
    upstream = lax.axis_index("section") == 0
    place, lane = lax.axis_index("seq"), lax.axis_index("tp")
    here, core = lane // CORES, lane % CORES
    tokens = kv_cotangent.shape[1]

    mixed = kv_cotangent[0].reshape(row, CORES, tokens // tp, -1)
    kept = lax.dynamic_index_in_dim(mixed, core, 1, keepdims=False)
    given = lax.dynamic_index_in_dim(mixed, 1 - core, 1, keepdims=False)
    given = over_cores(given)
    arrived = gather_seq(jnp.concatenate([kept, given], axis=2))
    cotangent = by_place(arrived)
    other = over_cores(kv_weight[0])
    weights = jnp.concatenate([kv_weight[0], other], axis=0)

    branch = mlp_grads[0].astype(jnp.float32)
    grad_one = output_cotangent.astype(jnp.float32) + branch
    behind = from_behind(mlp_grads[0], "section", -1)
    by_permutes = seq == tp == 2 * CORES
    gain = gain_slab(norm_gain)
    width = gain.shape[1]

    def kv_of(turn):
        part = lax.dynamic_index_in_dim(cotangent, (here + turn) % row, 1, keepdims=False)
        terms = jnp.dot(
            part.reshape(-1, part.shape[-1]), weights, preferred_element_type=jnp.float32
        )
        return terms.reshape(seq, tokens // tp, width)

    given = [kv_of(turn).astype(jnp.bfloat16) for turn in range(1, row)]
    residual = jnp.where(upstream, grad_one + after(behind, *given).astype(jnp.float32), grad_one)
    residual = after(residual.astype(jnp.bfloat16), *given)
    if by_permutes:
        near, far = slabs_by_permutes([layer_input[0]])
        values = collect(*spread(near, after(far, *given)))[:, 0]
    else:
        values = to_slabs(mix_tokens([layer_input[0]]))[:, 0]
    given = [over_rows(terms, turn) for turn, terms in enumerate(given, 1)]
    kv_share, values = lax.optimization_barrier((kv_of(0), values))
    for terms in given:
        kv_share = kv_share + terms.astype(jnp.float32)
    values = values.astype(jnp.float32)
    sums = local_sums(values, gain, kv_share)
    if by_permutes:
        near, far = slabs_by_permutes([residual])
        arrived, slot = spread(near, after(far, sums))
    norm_back = norm_backward(values, gain, kv_share, sums).astype(jnp.bfloat16)
    if by_permutes:
        base = collect(arrived, after(slot, norm_back))[:, 0]
    else:
        base = to_slabs(mix_tokens([residual]))[:, 0]

    depth = tokens // tp // CHUNKS

    def cut(array, c):
        return array[:, c * depth : (c + 1) * depth]

    leaving = [cut(norm_back, c) for c in range(CHUNKS)]
    arrivals = [from_behind(part, "section", -1) for part in leaving]
    home = mix_features(after(norm_back, leaving[-1]))
    arriving = jnp.concatenate(arrivals, axis=1).astype(jnp.float32)
    grad_zero = arriving + base.astype(jnp.float32)
    grad = jnp.where(upstream, grad_zero.astype(jnp.bfloat16), base)
    blocks_of = []
    for c in range(CHUNKS):
        part = cut(grad, c)
        blocks_of.append([over_rows(part, turn) if turn else part for turn in range(row)])
    attn_parts = []
    for c, blocks in enumerate(blocks_of):
        if c > 0:
            blocks[-1] = after(blocks[-1], attn_parts[-1][0])
        pieces = [half for block in blocks for half in (block, over_cores(block))]
        terms = product(pieces, out_weight[0])
        first = lax.dynamic_index_in_dim(terms, (place - 1) % seq, 0, keepdims=False)
        if c == 0:
            first = after(first, home)
        attn_parts.append([first, terms])
    home = exchange(after(home, attn_parts[-1][0]), "tp")
    home = home.reshape(tokens, -1).astype(jnp.float32)
    own = (grad_one + home).astype(jnp.bfloat16)
    arrived = from_behind(own, "section", -1)
    input_zero = (arrived.astype(jnp.float32) + branch + home).astype(jnp.bfloat16)
    input_part = jnp.where(upstream, input_zero, own)
    for c, (mine, terms) in enumerate(attn_parts):
        for step in range(2, seq + 1):
            total = lax.ppermute(mine, "seq", [(q, (q + 1) % seq) for q in range(seq)])
            if c == 0 and step == 3:
                total = after(total, own)
            if c == CHUNKS - 1 and step == seq:
                total = after(total, input_part)
            mine = lax.dynamic_index_in_dim(terms, (place - step) % seq, 0, keepdims=False)
            mine = mine.astype(jnp.float32) + total.astype(jnp.float32)
            mine = mine.astype(jnp.bfloat16)
        attn_parts[c] = mine
    attn_part = jnp.concatenate(attn_parts, axis=1)
    order = []
    for t in range(tp):
        which = (here - t // CORES) % row * CORES + (lane + t) % CORES
        order.append(lax.dynamic_index_in_dim(attn_part, which, 0, keepdims=False))
    attn_part = jnp.concatenate(order, axis=0)

    return (attn_part[None], input_part[None])


def solution(mesh):
    in_specs = (
        P("section", "seq", "tp"),
        P("section", "tp"),
        P("section", "seq", "tp"),
        P("section", "tp", "seq"),
        P("section", "seq", "tp"),
        P("seq", "tp"),
        P("section", "tp", "seq"),
    )
    out_specs = (P("section", "seq", "tp"), P("section", "seq", "tp"))
    return jax.shard_map(body, mesh=mesh, in_specs=in_specs, out_specs=out_specs, check_vma=False)
```

```python
import jax
import jax.numpy as jnp
from jax import lax
from jax.experimental import pallas as pl
from jax.experimental.pallas import tpu as pltpu
from jax.sharding import PartitionSpec as P

D = 8192


epsilon = 1e-05
CORES = 2
CHUNKS = 2


def from_behind(block, axis, distance):
    devices = range(lax.axis_size(axis))
    route = [(i - distance, i) for i in devices if i - distance in devices]
    return lax.ppermute(block, axis, route)


def after(value, *others):
    return lax.optimization_barrier((value, *others))[0]


def sizes():
    seq, tp = lax.axis_size("seq"), lax.axis_size("tp")
    assert seq % tp == 0 and tp % CORES == 0
    return seq, tp, seq // tp


def over_rows(block, turn):
    tp = lax.axis_size("tp")
    return lax.ppermute(block, "tp", [(t, (t + turn * CORES) % tp) for t in range(tp)])


def over_cores(block):
    tp = lax.axis_size("tp")
    return lax.ppermute(block, "tp", [(t, t ^ 1) for t in range(tp)])


def exchange(block, axis):
    return lax.all_to_all(block, axis, 0, 0)


def mix_tokens(blocks):
    tp = lax.axis_size("tp")
    tokens, width = blocks[0].shape
    stacked = jnp.stack([block.reshape(tp, tokens // tp, width) for block in blocks], axis=1)
    return exchange(stacked, "tp")


def to_slabs(parts):
    seq, tp, ratio = sizes()
    _, count, tokens, width = parts.shape
    if ratio > 1:
        parts = parts.reshape(tp, count, tokens, ratio, width // ratio).transpose(0, 3, 1, 2, 4)
    return exchange(parts.reshape(seq, count, tokens, width // ratio), "seq")


def slabs_by_permutes(blocks):
    seq, tp, _ = sizes()
    place, lane = lax.axis_index("seq"), lax.axis_index("tp")
    here, core = lane // CORES, lane % CORES
    tokens, width = blocks[0].shape
    stacked = jnp.stack(
        [block.reshape(tp // CORES, CORES, tokens // tp, width) for block in blocks], axis=2
    )
    near = lax.dynamic_index_in_dim(stacked, here, 0, keepdims=False)
    far = over_rows(lax.dynamic_index_in_dim(stacked, 1 - here, 0, keepdims=False), 1)
    return near, far


def spread(near, far):
    seq, tp, _ = sizes()
    place, lane = lax.axis_index("seq"), lax.axis_index("tp")
    here, core = lane // CORES, lane % CORES
    arrived = []
    for j in range(seq):
        slot = place ^ j
        piece = jnp.where(
            slot // CORES == here,
            lax.dynamic_index_in_dim(near, slot % CORES, 0, keepdims=False),
            lax.dynamic_index_in_dim(far, slot % CORES, 0, keepdims=False),
        )
        route = []
        for q in range(seq):
            for t in range(tp):
                to = (t % CORES + (q ^ j) // CORES * CORES, t // CORES * CORES + (q ^ j) % CORES)
                if to != (q, t):
                    route.append((q * tp + t, to[0] * tp + to[1]))
        moved = lax.ppermute(piece, ("seq", "tp"), route)
        if j == 0:
            moved = jnp.where(core == place % CORES, piece, moved)
        arrived.append(moved)
    return arrived, place // CORES * CORES + core


def collect(arrived, slot):
    return jnp.stack([lax.select_n(slot ^ q, *arrived) for q in range(len(arrived))], axis=0)


def mix_features(block):
    seq, tp, ratio = sizes()
    _, tokens, width = block.shape
    parts = exchange(block, "seq")
    if ratio > 1:
        parts = parts.reshape(tp, ratio, tokens, width).transpose(0, 2, 1, 3)
    return parts.reshape(tp, tokens, width * ratio)


def gain_slab(gain):
    seq, tp, ratio = sizes()
    place, lane = lax.axis_index("seq"), lax.axis_index("tp")
    width = gain.shape[1] // ratio
    own = lax.dynamic_slice_in_dim(gain, place % ratio * width, width, 1)
    route = []
    for q in range(seq):
        for t in range(tp):
            to = (t * ratio + q % ratio, q // ratio)
            if to != (q, t):
                route.append((q * tp + t, to[0] * tp + to[1]))
    moved = lax.ppermute(own, ("seq", "tp"), route)
    stays = (place == lane * ratio + place % ratio) & (lane == place // ratio)
    return jnp.where(stays, own, moved)


def gather_seq(block):
    seq = lax.axis_size("seq")
    place = lax.axis_index("seq")
    arrived = [block]
    for turn in range(1, seq):
        route = [(q, (q + turn) % seq) for q in range(seq)]
        arrived.append(lax.ppermute(block, "seq", route))
    return jnp.stack([lax.select_n((place - q) % seq, *arrived) for q in range(seq)], axis=0)


def local_sums(values, gain, kv_share):
    return jnp.stack([jnp.sum(values * values, axis=-1), jnp.sum(gain * kv_share * values, axis=-1)])


def norm_backward(values, gain, kv_share, sums):
    short = lax.axis_size("seq") <= 2 * CORES
    squares, intersection = jnp.sum(gather_seq(sums), axis=0) if short else lax.psum(sums, "seq")
    inv_rms = lax.rsqrt(squares / D + epsilon)[..., None]
    return (
        inv_rms * gain * kv_share
        - values * (inv_rms * inv_rms * inv_rms) * intersection[..., None] / D
    )


def product_kernel(*refs):
    *pieces, weight, out, rows = refs
    seq, depth, width = pieces[0].shape

    @pl.when(pl.program_id(0) == 0)
    def _():
        for i, piece in enumerate(pieces):
            rows[i] = piece[...]

    terms = lax.dot_general(
        rows[...].reshape(-1, width),
        weight[...],
        (((1,), (1,)), ((), ())),
        preferred_element_type=jnp.float32,
    ).astype(out.dtype)
    for i in range(len(pieces)):
        for q in range(seq):
            start = (i * seq + q) * depth
            out[q, i] = terms[start : start + depth]


def product(pieces, weight):
    seq, depth, width = pieces[0].shape
    heads = weight.shape[0]
    block = min(512, heads)
    n = len(pieces)
    return pl.pallas_call(
        product_kernel,
        out_shape=jax.ShapeDtypeStruct((seq, n, depth, heads), jnp.bfloat16),
        grid=(heads // block,),
        in_specs=[pl.BlockSpec((seq, depth, width), lambda i: (0, 0, 0)) for _ in pieces]
        + [pl.BlockSpec((block, width), lambda i: (i, 0))],
        out_specs=pl.BlockSpec((seq, n, depth, block), lambda i: (0, 0, 0, i)),
        cost_estimate=pl.CostEstimate(
            flops=2 * n * seq * depth * width * heads,
            bytes_accessed=2 * heads * width + 2 * n * seq * depth * heads,
            transcendentals=0,
        ),
        scratch_shapes=[pltpu.VMEM((n, seq, depth, width), pieces[0].dtype)],
        compiler_params=pltpu.CompilerParams(
            dimension_semantics=("arbitrary",), vmem_limit_bytes=44 * 1024 * 1024
        ),
    )(*pieces, weight)


def body(layer_input, norm_gain, kv_cotangent, kv_weight, mlp_grads, output_cotangent, out_weight):
    seq, tp, ratio = sizes()
    row = tp // CORES
    upstream = lax.axis_index("section") == 0
    place, lane = lax.axis_index("seq"), lax.axis_index("tp")
    here, core = lane // CORES, lane % CORES
    tokens = kv_cotangent.shape[1]

    mixed = kv_cotangent[0].reshape(row, CORES, tokens // tp, -1)
    kept = lax.dynamic_index_in_dim(mixed, core, 1, keepdims=False)
    given = lax.dynamic_index_in_dim(mixed, 1 - core, 1, keepdims=False)
    given = over_cores(given)
    cotangent = gather_seq(
        jnp.concatenate(
            [jnp.where(core == 0, kept, given), jnp.where(core == 0, given, kept)], axis=2
        )
    )
    pairs = [[t + core for core in range(CORES)] for t in range(0, tp, CORES)]
    weights = lax.all_gather(kv_weight[0], "tp", axis=0, axis_index_groups=pairs, tiled=True)

    branch = mlp_grads[0].astype(jnp.float32)
    grad_one = output_cotangent.astype(jnp.float32) + branch
    behind = from_behind(mlp_grads[0], "section", -1)
    by_permutes = seq == tp == 2 * CORES
    gain = gain_slab(norm_gain)
    width = gain.shape[1]

    def kv_of(turn):
        part = lax.dynamic_index_in_dim(cotangent, (here + turn) % row, 1, keepdims=False)
        terms = jnp.dot(
            part.reshape(-1, part.shape[-1]), weights, preferred_element_type=jnp.float32
        )
        return terms.reshape(seq, tokens // tp, width)

    given = [kv_of(turn).astype(jnp.bfloat16) for turn in range(1, row)]
    residual = jnp.where(upstream, grad_one + after(behind, *given).astype(jnp.float32), grad_one)
    residual = after(residual.astype(jnp.bfloat16), *given)
    if by_permutes:
        near, far = slabs_by_permutes([layer_input[0]])
        values = collect(*spread(near, after(far, *given)))[:, 0]
    else:
        values = to_slabs(mix_tokens([layer_input[0]]))[:, 0]
    given = [over_rows(terms, turn) for turn, terms in enumerate(given, 1)]
    kv_share, values = lax.optimization_barrier((kv_of(0), values))
    for terms in given:
        kv_share = kv_share + terms.astype(jnp.float32)
    values = values.astype(jnp.float32)
    sums = local_sums(values, gain, kv_share)
    if by_permutes:
        near, far = slabs_by_permutes([residual])
        arrived, slot = spread(near, after(far, sums))
    norm_back = norm_backward(values, gain, kv_share, sums).astype(jnp.bfloat16)
    if by_permutes:
        base = collect(arrived, after(slot, norm_back))[:, 0]
    else:
        base = to_slabs(mix_tokens([residual]))[:, 0]

    depth = tokens // tp // CHUNKS

    def cut(array, c):
        return array[:, c * depth : (c + 1) * depth]

    leaving = [cut(norm_back, c) for c in range(CHUNKS)]
    arrivals = [from_behind(part, "section", -1) for part in leaving]
    home = mix_features(after(norm_back, leaving[-1]))
    attn_parts = []
    for c in range(CHUNKS):
        part = cut(base, c)
        arriving = arrivals[c] if c == 0 else after(arrivals[c], attn_parts[-1][0])
        grad_zero = arriving.astype(jnp.float32) + part.astype(jnp.float32)
        grad = jnp.where(upstream, grad_zero.astype(jnp.bfloat16), part)
        blocks = [over_rows(grad, turn) if turn else grad for turn in range(row)]
        pieces = [half for block in blocks for half in (block, over_cores(block))]
        terms = product(pieces, out_weight[0])
        first = lax.dynamic_index_in_dim(terms, (place - 1) % seq, 0, keepdims=False)
        attn_parts.append([first, terms])
    attn_parts[0][0] = after(attn_parts[0][0], home)
    home = exchange(after(home, attn_parts[-1][0]), "tp")
    home = home.reshape(tokens, -1).astype(jnp.float32)
    own = (grad_one + home).astype(jnp.bfloat16)
    arrived = from_behind(own, "section", -1)
    input_zero = (arrived.astype(jnp.float32) + branch + home).astype(jnp.bfloat16)
    input_part = jnp.where(upstream, input_zero, own)
    for c, (mine, terms) in enumerate(attn_parts):
        for step in range(2, seq + 1):
            total = lax.ppermute(mine, "seq", [(q, (q + 1) % seq) for q in range(seq)])
            if c == 0 and step == 3:
                total = after(total, own)
            if c == CHUNKS - 1 and step == seq:
                total = after(total, input_part)
            mine = lax.dynamic_index_in_dim(terms, (place - step) % seq, 0, keepdims=False)
            mine = mine.astype(jnp.float32) + total.astype(jnp.float32)
            mine = mine.astype(jnp.bfloat16)
        attn_parts[c] = mine
    attn_part = jnp.concatenate(attn_parts, axis=1)
    order = []
    for t in range(tp):
        which = (here - t // CORES) % row * CORES + (lane + t) % CORES
        order.append(lax.dynamic_index_in_dim(attn_part, which, 0, keepdims=False))
    attn_part = jnp.concatenate(order, axis=0)

    return (attn_part[None], input_part[None])


def solution(mesh):
    in_specs = (
        P("section", "seq", "tp"),
        P("section", "tp"),
        P("section", "seq", "tp"),
        P("section", "tp", "seq"),
        P("section", "seq", "tp"),
        P("seq", "tp"),
        P("section", "tp", "seq"),
    )
    out_specs = (P("section", "seq", "tp"), P("section", "seq", "tp"))
    return jax.shard_map(body, mesh=mesh, in_specs=in_specs, out_specs=out_specs, check_vma=False)
```

```python
import jax
import jax.numpy as jnp
from jax import lax
from jax.experimental import pallas as pl
from jax.experimental.pallas import tpu as pltpu
from jax.sharding import PartitionSpec as P

D = 8192


epsilon = 1e-05
CORES = 2
CHUNKS = 2


def from_behind(block, axis, distance):
    devices = range(lax.axis_size(axis))
    route = [(i - distance, i) for i in devices if i - distance in devices]
    return lax.ppermute(block, axis, route)


def after(value, *others):
    return lax.optimization_barrier((value, *others))[0]


def sizes():
    seq, tp = lax.axis_size("seq"), lax.axis_size("tp")
    assert seq % tp == 0 and tp % CORES == 0
    return seq, tp, seq // tp


def over_rows(block, turn):
    tp = lax.axis_size("tp")
    return lax.ppermute(block, "tp", [(t, (t + turn * CORES) % tp) for t in range(tp)])


def over_cores(block):
    tp = lax.axis_size("tp")
    return lax.ppermute(block, "tp", [(t, t ^ 1) for t in range(tp)])


def exchange(block, axis):
    return lax.all_to_all(block, axis, 0, 0)


def mix_tokens(blocks):
    tp = lax.axis_size("tp")
    tokens, width = blocks[0].shape
    stacked = jnp.stack([block.reshape(tp, tokens // tp, width) for block in blocks], axis=1)
    return exchange(stacked, "tp")


def to_slabs(parts):
    seq, tp, ratio = sizes()
    _, count, tokens, width = parts.shape
    if ratio > 1:
        parts = parts.reshape(tp, count, tokens, ratio, width // ratio).transpose(0, 3, 1, 2, 4)
    return exchange(parts.reshape(seq, count, tokens, width // ratio), "seq")


def slabs_by_permutes(blocks):
    seq, tp, _ = sizes()
    place, lane = lax.axis_index("seq"), lax.axis_index("tp")
    here, core = lane // CORES, lane % CORES
    tokens, width = blocks[0].shape
    stacked = jnp.stack(
        [block.reshape(tp // CORES, CORES, tokens // tp, width) for block in blocks], axis=2
    )
    near = lax.dynamic_index_in_dim(stacked, here, 0, keepdims=False)
    far = over_rows(lax.dynamic_index_in_dim(stacked, 1 - here, 0, keepdims=False), 1)
    return near, far


def spread(near, far):
    seq, tp, _ = sizes()
    place, lane = lax.axis_index("seq"), lax.axis_index("tp")
    here, core = lane // CORES, lane % CORES
    arrived = []
    for j in range(seq):
        slot = place ^ j
        piece = jnp.where(
            slot // CORES == here,
            lax.dynamic_index_in_dim(near, slot % CORES, 0, keepdims=False),
            lax.dynamic_index_in_dim(far, slot % CORES, 0, keepdims=False),
        )
        route = []
        for q in range(seq):
            for t in range(tp):
                to = (t % CORES + (q ^ j) // CORES * CORES, t // CORES * CORES + (q ^ j) % CORES)
                if to != (q, t):
                    route.append((q * tp + t, to[0] * tp + to[1]))
        moved = lax.ppermute(piece, ("seq", "tp"), route)
        if j == 0:
            moved = jnp.where(core == place % CORES, piece, moved)
        arrived.append(moved)
    return arrived, place // CORES * CORES + core


def collect(arrived, slot):
    return jnp.stack([lax.select_n(slot ^ q, *arrived) for q in range(len(arrived))], axis=0)


def mix_features(block):
    seq, tp, ratio = sizes()
    _, tokens, width = block.shape
    parts = exchange(block, "seq")
    if ratio > 1:
        parts = parts.reshape(tp, ratio, tokens, width).transpose(0, 2, 1, 3)
    return parts.reshape(tp, tokens, width * ratio)


def gain_slab(gain):
    seq, tp, ratio = sizes()
    place, lane = lax.axis_index("seq"), lax.axis_index("tp")
    width = gain.shape[1] // ratio
    own = lax.dynamic_slice_in_dim(gain, place % ratio * width, width, 1)
    route = []
    for q in range(seq):
        for t in range(tp):
            to = (t * ratio + q % ratio, q // ratio)
            if to != (q, t):
                route.append((q * tp + t, to[0] * tp + to[1]))
    moved = lax.ppermute(own, ("seq", "tp"), route)
    stays = (place == lane * ratio + place % ratio) & (lane == place // ratio)
    return jnp.where(stays, own, moved)


def gather_seq(block):
    seq = lax.axis_size("seq")
    place = lax.axis_index("seq")
    arrived = [block]
    for turn in range(1, seq):
        route = [(q, (q + turn) % seq) for q in range(seq)]
        arrived.append(lax.ppermute(block, "seq", route))
    return jnp.stack([lax.select_n((place - q) % seq, *arrived) for q in range(seq)], axis=0)


def local_sums(values, gain, kv_share):
    return jnp.stack([jnp.sum(values * values, axis=-1), jnp.sum(gain * kv_share * values, axis=-1)])


def norm_backward(values, gain, kv_share, sums):
    short = lax.axis_size("seq") <= 2 * CORES
    squares, intersection = jnp.sum(gather_seq(sums), axis=0) if short else lax.psum(sums, "seq")
    inv_rms = lax.rsqrt(squares / D + epsilon)[..., None]
    return (
        inv_rms * gain * kv_share
        - values * (inv_rms * inv_rms * inv_rms) * intersection[..., None] / D
    )


def product_kernel(*refs):
    *pieces, weight, out, rows = refs
    seq, depth, width = pieces[0].shape

    @pl.when(pl.program_id(0) == 0)
    def _():
        for i, piece in enumerate(pieces):
            rows[i] = piece[...]

    terms = lax.dot_general(
        rows[...].reshape(-1, width),
        weight[...],
        (((1,), (1,)), ((), ())),
        preferred_element_type=jnp.float32,
    ).astype(out.dtype)
    for i in range(len(pieces)):
        for q in range(seq):
            start = (i * seq + q) * depth
            out[q, i] = terms[start : start + depth]


def product(pieces, weight):
    seq, depth, width = pieces[0].shape
    heads = weight.shape[0]
    block = min(512, heads)
    n = len(pieces)
    return pl.pallas_call(
        product_kernel,
        out_shape=jax.ShapeDtypeStruct((seq, n, depth, heads), jnp.bfloat16),
        grid=(heads // block,),
        in_specs=[pl.BlockSpec((seq, depth, width), lambda i: (0, 0, 0)) for _ in pieces]
        + [pl.BlockSpec((block, width), lambda i: (i, 0))],
        out_specs=pl.BlockSpec((seq, n, depth, block), lambda i: (0, 0, 0, i)),
        cost_estimate=pl.CostEstimate(
            flops=2 * n * seq * depth * width * heads,
            bytes_accessed=2 * heads * width + 2 * n * seq * depth * heads,
            transcendentals=0,
        ),
        scratch_shapes=[pltpu.VMEM((n, seq, depth, width), pieces[0].dtype)],
        compiler_params=pltpu.CompilerParams(
            dimension_semantics=("arbitrary",), vmem_limit_bytes=32 * 1024 * 1024
        ),
    )(*pieces, weight)


def body(layer_input, norm_gain, kv_cotangent, kv_weight, mlp_grads, output_cotangent, out_weight):
    seq, tp, ratio = sizes()
    row = tp // CORES
    upstream = lax.axis_index("section") == 0
    place, lane = lax.axis_index("seq"), lax.axis_index("tp")
    here, core = lane // CORES, lane % CORES
    tokens = kv_cotangent.shape[1]

    mixed = kv_cotangent[0].reshape(row, CORES, tokens // tp, -1)
    kept = lax.dynamic_index_in_dim(mixed, core, 1, keepdims=False)
    given = lax.dynamic_index_in_dim(mixed, 1 - core, 1, keepdims=False)
    given = over_cores(given)
    cotangent = jnp.concatenate([kept, given], axis=2)
    mlp = after(mlp_grads[0], cotangent)
    cotangent = gather_seq(cotangent)
    weights = jnp.concatenate([kv_weight[0], over_cores(kv_weight[0])], axis=0)

    branch = mlp_grads[0].astype(jnp.float32)
    grad_one = output_cotangent.astype(jnp.float32) + branch
    behind = from_behind(mlp, "section", -1)
    by_permutes = seq == tp == 2 * CORES
    gain = gain_slab(norm_gain)
    width = gain.shape[1]

    def kv_of(turn):
        part = lax.dynamic_index_in_dim(cotangent, (here + turn) % row, 1, keepdims=False)
        terms = jnp.dot(
            part.reshape(-1, part.shape[-1]), weights, preferred_element_type=jnp.float32
        )
        return terms.reshape(seq, tokens // tp, width)

    given = [kv_of(turn).astype(jnp.bfloat16) for turn in range(1, row)]
    residual = jnp.where(upstream, grad_one + after(behind, *given).astype(jnp.float32), grad_one)
    residual = after(residual.astype(jnp.bfloat16), *given)
    if by_permutes:
        near, far = slabs_by_permutes([layer_input[0]])
        values = collect(*spread(near, after(far, *given)))[:, 0]
    else:
        values = to_slabs(mix_tokens([layer_input[0]]))[:, 0]
    given = [over_rows(terms, turn) for turn, terms in enumerate(given, 1)]
    kv_share, values = lax.optimization_barrier((kv_of(0), values))
    for terms in given:
        kv_share = kv_share + terms.astype(jnp.float32)
    values = values.astype(jnp.float32)
    sums = local_sums(values, gain, kv_share)
    if by_permutes:
        near, far = slabs_by_permutes([residual])
        arrived, slot = spread(near, after(far, sums))
    norm_back = norm_backward(values, gain, kv_share, sums).astype(jnp.bfloat16)
    if by_permutes:
        base = collect(arrived, after(slot, norm_back))[:, 0]
    else:
        base = to_slabs(mix_tokens([residual]))[:, 0]

    depth = tokens // tp // CHUNKS

    def cut(array, c):
        return array[:, c * depth : (c + 1) * depth]

    leaving = [cut(norm_back, c) for c in range(CHUNKS)]
    arrivals = [from_behind(part, "section", -1) for part in leaving]
    home = mix_features(after(norm_back, leaving[-1]))
    blocks_of = []
    for c in range(CHUNKS):
        part = cut(base, c)
        arriving = arrivals[c]
        if c > 0:
            arriving = after(arriving, blocks[-1])
        grad_zero = arriving.astype(jnp.float32) + part.astype(jnp.float32)
        grad = jnp.where(upstream, grad_zero.astype(jnp.bfloat16), part)
        blocks = [over_rows(grad, turn) if turn else grad for turn in range(row)]
        blocks_of.append(blocks)
    attn_parts = []
    for c, blocks in enumerate(blocks_of):
        if c > 0:
            blocks[-1] = after(blocks[-1], attn_parts[-1][0])
        pieces = [half for block in blocks for half in (block, over_cores(block))]
        terms = product(pieces, out_weight[0])
        first = lax.dynamic_index_in_dim(terms, (place - 1) % seq, 0, keepdims=False)
        if c == 0:
            first = after(first, home)
        attn_parts.append([first, terms])
    home = exchange(after(home, attn_parts[-1][0]), "tp")
    home = home.reshape(tokens, -1).astype(jnp.float32)
    own = (grad_one + home).astype(jnp.bfloat16)
    arrived = from_behind(own, "section", -1)
    input_zero = (arrived.astype(jnp.float32) + branch + home).astype(jnp.bfloat16)
    input_part = jnp.where(upstream, input_zero, own)
    for c, (mine, terms) in enumerate(attn_parts):
        for step in range(2, seq + 1):
            total = lax.ppermute(mine, "seq", [(q, (q + 1) % seq) for q in range(seq)])
            if c == 0 and step == 3:
                total = after(total, own)
            if c == CHUNKS - 1 and step == seq:
                total = after(total, input_part)
            mine = lax.dynamic_index_in_dim(terms, (place - step) % seq, 0, keepdims=False)
            mine = mine.astype(jnp.float32) + total.astype(jnp.float32)
            mine = mine.astype(jnp.bfloat16)
        attn_parts[c] = mine
    attn_part = jnp.concatenate(attn_parts, axis=1)
    order = []
    for t in range(tp):
        which = (here - t // CORES) % row * CORES + (lane + t) % CORES
        order.append(lax.dynamic_index_in_dim(attn_part, which, 0, keepdims=False))
    attn_part = jnp.concatenate(order, axis=0)

    return (attn_part[None], input_part[None])


def solution(mesh):
    in_specs = (
        P("section", "seq", "tp"),
        P("section", "tp"),
        P("section", "seq", "tp"),
        P("section", "tp", "seq"),
        P("section", "seq", "tp"),
        P("seq", "tp"),
        P("section", "tp", "seq"),
    )
    out_specs = (P("section", "seq", "tp"), P("section", "seq", "tp"))
    return jax.shard_map(body, mesh=mesh, in_specs=in_specs, out_specs=out_specs, check_vma=False)
```

```python
import jax
import jax.numpy as jnp
from jax import lax
from jax.sharding import PartitionSpec as P

D = 8192


epsilon = 1e-05
CORES = 2
CHUNKS = 2


def from_behind(block, axis, distance):
    devices = range(lax.axis_size(axis))
    route = [(i - distance, i) for i in devices if i - distance in devices]
    return lax.ppermute(block, axis, route)


def after(value, *others):
    return lax.optimization_barrier((value, *others))[0]


def sizes():
    seq, tp = lax.axis_size("seq"), lax.axis_size("tp")
    assert seq % tp == 0 and tp % CORES == 0
    return seq, tp, seq // tp


def over_rows(block, turn):
    tp = lax.axis_size("tp")
    return lax.ppermute(block, "tp", [(t, (t + turn * CORES) % tp) for t in range(tp)])


def over_cores(block):
    tp = lax.axis_size("tp")
    return lax.ppermute(block, "tp", [(t, t ^ 1) for t in range(tp)])


def exchange(block, axis):
    return lax.all_to_all(block, axis, 0, 0)


def mix_tokens(blocks):
    tp = lax.axis_size("tp")
    tokens, width = blocks[0].shape
    stacked = jnp.stack([block.reshape(tp, tokens // tp, width) for block in blocks], axis=1)
    return exchange(stacked, "tp")


def to_slabs(parts):
    seq, tp, ratio = sizes()
    _, count, tokens, width = parts.shape
    if ratio > 1:
        parts = parts.reshape(tp, count, tokens, ratio, width // ratio).transpose(0, 3, 1, 2, 4)
    return exchange(parts.reshape(seq, count, tokens, width // ratio), "seq")


def slabs_by_permutes(blocks):
    seq, tp, _ = sizes()
    place, lane = lax.axis_index("seq"), lax.axis_index("tp")
    here, core = lane // CORES, lane % CORES
    tokens, width = blocks[0].shape
    stacked = jnp.stack(
        [block.reshape(tp // CORES, CORES, tokens // tp, width) for block in blocks], axis=2
    )
    near = lax.dynamic_index_in_dim(stacked, here, 0, keepdims=False)
    far = over_rows(lax.dynamic_index_in_dim(stacked, 1 - here, 0, keepdims=False), 1)
    return near, far


def spread(near, far):
    seq, tp, _ = sizes()
    place, lane = lax.axis_index("seq"), lax.axis_index("tp")
    here, core = lane // CORES, lane % CORES
    arrived = []
    for j in range(seq):
        slot = place ^ j
        piece = jnp.where(
            slot // CORES == here,
            lax.dynamic_index_in_dim(near, slot % CORES, 0, keepdims=False),
            lax.dynamic_index_in_dim(far, slot % CORES, 0, keepdims=False),
        )
        route = []
        for q in range(seq):
            for t in range(tp):
                to = (t % CORES + (q ^ j) // CORES * CORES, t // CORES * CORES + (q ^ j) % CORES)
                if to != (q, t):
                    route.append((q * tp + t, to[0] * tp + to[1]))
        moved = lax.ppermute(piece, ("seq", "tp"), route)
        if j == 0:
            moved = jnp.where(core == place % CORES, piece, moved)
        arrived.append(moved)
    return arrived, place // CORES * CORES + core


def collect(arrived, slot):
    return jnp.stack([lax.select_n(slot ^ q, *arrived) for q in range(len(arrived))], axis=0)


def mix_features(block):
    seq, tp, ratio = sizes()
    _, tokens, width = block.shape
    parts = exchange(block, "seq")
    if ratio > 1:
        parts = parts.reshape(tp, ratio, tokens, width).transpose(0, 2, 1, 3)
    return parts.reshape(tp, tokens, width * ratio)


def gain_slab(gain):
    seq, tp, ratio = sizes()
    place, lane = lax.axis_index("seq"), lax.axis_index("tp")
    width = gain.shape[1] // ratio
    own = lax.dynamic_slice_in_dim(gain, place % ratio * width, width, 1)
    route = []
    for q in range(seq):
        for t in range(tp):
            to = (t * ratio + q % ratio, q // ratio)
            if to != (q, t):
                route.append((q * tp + t, to[0] * tp + to[1]))
    moved = lax.ppermute(own, ("seq", "tp"), route)
    stays = (place == lane * ratio + place % ratio) & (lane == place // ratio)
    return jnp.where(stays, own, moved)


def gather_seq(block):
    seq = lax.axis_size("seq")
    place = lax.axis_index("seq")
    arrived = [block]
    for turn in range(1, seq):
        route = [(q, (q + turn) % seq) for q in range(seq)]
        arrived.append(lax.ppermute(block, "seq", route))
    return jnp.stack([lax.select_n((place - q) % seq, *arrived) for q in range(seq)], axis=0)


def local_sums(values, gain, kv_share):
    return jnp.stack([jnp.sum(values * values, axis=-1), jnp.sum(gain * kv_share * values, axis=-1)])


def norm_backward(values, gain, kv_share, sums):
    short = lax.axis_size("seq") <= 2 * CORES
    squares, intersection = jnp.sum(gather_seq(sums), axis=0) if short else lax.psum(sums, "seq")
    inv_rms = lax.rsqrt(squares / D + epsilon)[..., None]
    return (
        inv_rms * gain * kv_share
        - values * (inv_rms * inv_rms * inv_rms) * intersection[..., None] / D
    )


def product(piece, weight):
    terms = lax.dot_general(
        piece, weight, (((2,), (1,)), ((), ())), preferred_element_type=jnp.float32
    )
    return terms.astype(jnp.bfloat16)


def pick(terms, at):
    return jnp.stack([lax.dynamic_index_in_dim(part, at, 0, keepdims=False) for part in terms], axis=0)


def body(layer_input, norm_gain, kv_cotangent, kv_weight, mlp_grads, output_cotangent, out_weight):
    seq, tp, ratio = sizes()
    row = tp // CORES
    upstream = lax.axis_index("section") == 0
    place, lane = lax.axis_index("seq"), lax.axis_index("tp")
    here, core = lane // CORES, lane % CORES
    tokens = kv_cotangent.shape[1]

    mixed = kv_cotangent[0].reshape(row, CORES, tokens // tp, -1)
    kept = lax.dynamic_index_in_dim(mixed, core, 1, keepdims=False)
    given = lax.dynamic_index_in_dim(mixed, 1 - core, 1, keepdims=False)
    given = over_cores(given)
    cotangent = jnp.concatenate([kept, given], axis=2)
    mlp = after(mlp_grads[0], cotangent)
    cotangent = gather_seq(cotangent)
    weights = jnp.concatenate([kv_weight[0], over_cores(kv_weight[0])], axis=0)

    branch = mlp_grads[0].astype(jnp.float32)
    grad_one = output_cotangent.astype(jnp.float32) + branch
    behind = from_behind(mlp, "section", -1)
    by_permutes = seq == tp == 2 * CORES
    gain = gain_slab(norm_gain)
    width = gain.shape[1]

    def kv_of(turn):
        part = lax.dynamic_index_in_dim(cotangent, (here + turn) % row, 1, keepdims=False)
        terms = jnp.dot(
            part.reshape(-1, part.shape[-1]), weights, preferred_element_type=jnp.float32
        )
        return terms.reshape(seq, tokens // tp, width)

    given = [kv_of(turn).astype(jnp.bfloat16) for turn in range(1, row)]
    residual = jnp.where(upstream, grad_one + after(behind, *given).astype(jnp.float32), grad_one)
    residual = after(residual.astype(jnp.bfloat16), *given)
    if by_permutes:
        near, far = slabs_by_permutes([layer_input[0]])
        values = collect(*spread(near, after(far, *given)))[:, 0]
    else:
        values = to_slabs(mix_tokens([layer_input[0]]))[:, 0]
    given = [over_rows(terms, turn) for turn, terms in enumerate(given, 1)]
    kv_share, values = lax.optimization_barrier((kv_of(0), values))
    for terms in given:
        kv_share = kv_share + terms.astype(jnp.float32)
    values = values.astype(jnp.float32)
    sums = local_sums(values, gain, kv_share)
    if by_permutes:
        near, far = slabs_by_permutes([residual])
        arrived, slot = spread(near, after(far, sums))
    norm_back = norm_backward(values, gain, kv_share, sums).astype(jnp.bfloat16)
    if by_permutes:
        base = collect(arrived, after(slot, norm_back))[:, 0]
    else:
        base = to_slabs(mix_tokens([residual]))[:, 0]

    depth = tokens // tp // CHUNKS

    def cut(array, c):
        return array[:, c * depth : (c + 1) * depth]

    leaving = [cut(norm_back, c) for c in range(CHUNKS)]
    if by_permutes:
        leaving[1:] = [after(part, arrived[0]) for part in leaving[1:]]
    arrivals = [from_behind(part, "section", -1) for part in leaving]
    home = mix_features(after(norm_back, leaving[0]))
    pieces_of = []
    for c in range(CHUNKS):
        part = cut(base, c)
        arriving = arrivals[c] if c == 0 else after(arrivals[c], pieces_of[-1][-1])
        grad_zero = arriving.astype(jnp.float32) + part.astype(jnp.float32)
        grad = jnp.where(upstream, grad_zero.astype(jnp.bfloat16), part)
        blocks = [over_rows(grad, turn) if turn else grad for turn in range(row)]
        pieces_of.append([half for block in blocks for half in (block, over_cores(block))])
    attn_parts = []
    for c, pieces in enumerate(pieces_of):
        if c > 0:
            pieces = [after(piece, attn_parts[-1][0]) for piece in pieces]
        terms = []
        for piece in pieces:
            terms.append(product(after(piece, *terms[-1:]), out_weight[0]))
        first = pick(terms, (place - 1) % seq)
        if c == 0:
            first = after(first, home)
        attn_parts.append([first, terms])
    home = exchange(after(home, attn_parts[-1][0]), "tp")
    home = home.reshape(tokens, -1).astype(jnp.float32)
    own = (grad_one + home).astype(jnp.bfloat16)
    arrived = from_behind(own, "section", -1)
    input_zero = (arrived.astype(jnp.float32) + branch + home).astype(jnp.bfloat16)
    input_part = jnp.where(upstream, input_zero, own)
    for c, (mine, terms) in enumerate(attn_parts):
        for step in range(2, seq + 1):
            total = lax.ppermute(mine, "seq", [(q, (q + 1) % seq) for q in range(seq)])
            if c == 0 and step == 3:
                total = after(total, own)
            if c == CHUNKS - 1 and step == seq:
                total = after(total, input_part)
            mine = pick(terms, (place - step) % seq)
            mine = mine.astype(jnp.float32) + total.astype(jnp.float32)
            mine = mine.astype(jnp.bfloat16)
        attn_parts[c] = mine
    attn_part = jnp.concatenate(attn_parts, axis=1)
    order = []
    for t in range(tp):
        which = (here - t // CORES) % row * CORES + (lane + t) % CORES
        order.append(lax.dynamic_index_in_dim(attn_part, which, 0, keepdims=False))
    attn_part = jnp.concatenate(order, axis=0)

    return (attn_part[None], input_part[None])


def solution(mesh):
    in_specs = (
        P("section", "seq", "tp"),
        P("section", "tp"),
        P("section", "seq", "tp"),
        P("section", "tp", "seq"),
        P("section", "seq", "tp"),
        P("seq", "tp"),
        P("section", "tp", "seq"),
    )
    out_specs = (P("section", "seq", "tp"), P("section", "seq", "tp"))
    return jax.shard_map(body, mesh=mesh, in_specs=in_specs, out_specs=out_specs, check_vma=False)
```

```python
import jax
import jax.numpy as jnp
from jax import lax
from jax.experimental import pallas as pl
from jax.experimental.pallas import tpu as pltpu
from jax.sharding import PartitionSpec as P

D = 8192


epsilon = 1e-05
CORES = 2
CHUNKS = 2


def from_behind(block, axis, distance):
    devices = range(lax.axis_size(axis))
    route = [(i - distance, i) for i in devices if i - distance in devices]
    return lax.ppermute(block, axis, route)


def after(value, *others):
    return lax.optimization_barrier((value, *others))[0]


def sizes():
    seq, tp = lax.axis_size("seq"), lax.axis_size("tp")
    assert seq % tp == 0 and tp % CORES == 0
    return seq, tp, seq // tp


def over_rows(block, turn):
    tp = lax.axis_size("tp")
    return lax.ppermute(block, "tp", [(t, (t + turn * CORES) % tp) for t in range(tp)])


def over_cores(block):
    tp = lax.axis_size("tp")
    return lax.ppermute(block, "tp", [(t, t ^ 1) for t in range(tp)])


def exchange(block, axis):
    return lax.all_to_all(block, axis, 0, 0)


def mix_tokens(blocks):
    tp = lax.axis_size("tp")
    tokens, width = blocks[0].shape
    stacked = jnp.stack([block.reshape(tp, tokens // tp, width) for block in blocks], axis=1)
    return exchange(stacked, "tp")


def to_slabs(parts):
    seq, tp, ratio = sizes()
    _, count, tokens, width = parts.shape
    if ratio > 1:
        parts = parts.reshape(tp, count, tokens, ratio, width // ratio).transpose(0, 3, 1, 2, 4)
    return exchange(parts.reshape(seq, count, tokens, width // ratio), "seq")


def slabs_by_permutes(blocks):
    seq, tp, _ = sizes()
    place, lane = lax.axis_index("seq"), lax.axis_index("tp")
    here, core = lane // CORES, lane % CORES
    tokens, width = blocks[0].shape
    stacked = jnp.stack(
        [block.reshape(tp // CORES, CORES, tokens // tp, width) for block in blocks], axis=2
    )
    near = lax.dynamic_index_in_dim(stacked, here, 0, keepdims=False)
    far = over_rows(lax.dynamic_index_in_dim(stacked, 1 - here, 0, keepdims=False), 1)
    return near, far


def spread(near, far):
    seq, tp, _ = sizes()
    place, lane = lax.axis_index("seq"), lax.axis_index("tp")
    here, core = lane // CORES, lane % CORES
    arrived = []
    for j in range(seq):
        slot = place ^ j
        piece = jnp.where(
            slot // CORES == here,
            lax.dynamic_index_in_dim(near, slot % CORES, 0, keepdims=False),
            lax.dynamic_index_in_dim(far, slot % CORES, 0, keepdims=False),
        )
        route = []
        for q in range(seq):
            for t in range(tp):
                to = (t % CORES + (q ^ j) // CORES * CORES, t // CORES * CORES + (q ^ j) % CORES)
                if to != (q, t):
                    route.append((q * tp + t, to[0] * tp + to[1]))
        moved = lax.ppermute(piece, ("seq", "tp"), route)
        if j == 0:
            moved = jnp.where(core == place % CORES, piece, moved)
        arrived.append(moved)
    return arrived, place // CORES * CORES + core


def collect(arrived, slot):
    return jnp.stack([lax.select_n(slot ^ q, *arrived) for q in range(len(arrived))], axis=0)


def mix_features(block):
    seq, tp, ratio = sizes()
    _, tokens, width = block.shape
    parts = exchange(block, "seq")
    if ratio > 1:
        parts = parts.reshape(tp, ratio, tokens, width).transpose(0, 2, 1, 3)
    return parts.reshape(tp, tokens, width * ratio)


def gain_slab(gain):
    seq, tp, ratio = sizes()
    place, lane = lax.axis_index("seq"), lax.axis_index("tp")
    width = gain.shape[1] // ratio
    own = lax.dynamic_slice_in_dim(gain, place % ratio * width, width, 1)
    route = []
    for q in range(seq):
        for t in range(tp):
            to = (t * ratio + q % ratio, q // ratio)
            if to != (q, t):
                route.append((q * tp + t, to[0] * tp + to[1]))
    moved = lax.ppermute(own, ("seq", "tp"), route)
    stays = (place == lane * ratio + place % ratio) & (lane == place // ratio)
    return jnp.where(stays, own, moved)


def gather_seq(block):
    seq = lax.axis_size("seq")
    place = lax.axis_index("seq")
    arrived = [block]
    for turn in range(1, seq):
        route = [(q, (q + turn) % seq) for q in range(seq)]
        arrived.append(lax.ppermute(block, "seq", route))
    return jnp.stack([lax.select_n((place - q) % seq, *arrived) for q in range(seq)], axis=0)


def local_sums(values, gain, kv_share):
    return jnp.stack([jnp.sum(values * values, axis=-1), jnp.sum(gain * kv_share * values, axis=-1)])


def norm_backward(values, gain, kv_share, sums):
    short = lax.axis_size("seq") <= 2 * CORES
    squares, intersection = jnp.sum(gather_seq(sums), axis=0) if short else lax.psum(sums, "seq")
    inv_rms = lax.rsqrt(squares / D + epsilon)[..., None]
    return (
        inv_rms * gain * kv_share
        - values * (inv_rms * inv_rms * inv_rms) * intersection[..., None] / D
    )


def product_kernel(rows, weight, out):
    n, seq, depth, width = rows.shape
    terms = lax.dot_general(
        rows[...].reshape(-1, width),
        weight[...],
        (((1,), (1,)), ((), ())),
        preferred_element_type=jnp.float32,
    ).astype(out.dtype)
    for i in range(n):
        for q in range(seq):
            start = (i * seq + q) * depth
            out[q, i] = terms[start : start + depth]


def product(pieces, weight):
    rows = jnp.stack(pieces, axis=0)
    n, seq, depth, width = rows.shape
    heads = weight.shape[0]
    block = min(512, heads)
    return pl.pallas_call(
        product_kernel,
        out_shape=jax.ShapeDtypeStruct((seq, n, depth, heads), jnp.bfloat16),
        grid=(heads // block,),
        in_specs=[
            pl.BlockSpec((n, seq, depth, width), lambda i: (0, 0, 0, 0)),
            pl.BlockSpec((block, width), lambda i: (i, 0)),
        ],
        out_specs=pl.BlockSpec((seq, n, depth, block), lambda i: (0, 0, 0, i)),
        cost_estimate=pl.CostEstimate(
            flops=2 * n * seq * depth * width * heads,
            bytes_accessed=2 * heads * width + 2 * n * seq * depth * heads,
            transcendentals=0,
        ),
        compiler_params=pltpu.CompilerParams(
            dimension_semantics=("arbitrary",), vmem_limit_bytes=44 * 1024 * 1024
        ),
    )(rows, weight)


def body(layer_input, norm_gain, kv_cotangent, kv_weight, mlp_grads, output_cotangent, out_weight):
    seq, tp, ratio = sizes()
    row = tp // CORES
    upstream = lax.axis_index("section") == 0
    place, lane = lax.axis_index("seq"), lax.axis_index("tp")
    here, core = lane // CORES, lane % CORES
    tokens = kv_cotangent.shape[1]

    mixed = kv_cotangent[0].reshape(row, CORES, tokens // tp, -1)
    kept = lax.dynamic_index_in_dim(mixed, core, 1, keepdims=False)
    given = lax.dynamic_index_in_dim(mixed, 1 - core, 1, keepdims=False)
    given = over_cores(given)
    cotangent = jnp.concatenate([kept, given], axis=2)
    mlp = after(mlp_grads[0], cotangent)
    cotangent = gather_seq(cotangent)
    weights = jnp.concatenate([kv_weight[0], over_cores(kv_weight[0])], axis=0)

    branch = mlp_grads[0].astype(jnp.float32)
    grad_one = output_cotangent.astype(jnp.float32) + branch
    behind = from_behind(mlp, "section", -1)
    by_permutes = seq == tp == 2 * CORES
    gain = gain_slab(norm_gain)
    width = gain.shape[1]

    def kv_of(turn):
        part = lax.dynamic_index_in_dim(cotangent, (here + turn) % row, 1, keepdims=False)
        terms = jnp.dot(
            part.reshape(-1, part.shape[-1]), weights, preferred_element_type=jnp.float32
        )
        return terms.reshape(seq, tokens // tp, width)

    given = [kv_of(turn).astype(jnp.bfloat16) for turn in range(1, row)]
    residual = jnp.where(upstream, grad_one + after(behind, *given).astype(jnp.float32), grad_one)
    residual = after(residual.astype(jnp.bfloat16), *given)
    if by_permutes:
        near, far = slabs_by_permutes([layer_input[0]])
        values = collect(*spread(near, after(far, *given)))[:, 0]
    else:
        values = to_slabs(mix_tokens([layer_input[0]]))[:, 0]
    given = [over_rows(terms, turn) for turn, terms in enumerate(given, 1)]
    kv_share, values = lax.optimization_barrier((kv_of(0), values))
    for terms in given:
        kv_share = kv_share + terms.astype(jnp.float32)
    values = values.astype(jnp.float32)
    sums = local_sums(values, gain, kv_share)
    if by_permutes:
        near, far = slabs_by_permutes([residual])
        arrived, slot = spread(near, after(far, sums))
    norm_back = norm_backward(values, gain, kv_share, sums).astype(jnp.bfloat16)
    if by_permutes:
        base = collect(arrived, after(slot, norm_back))[:, 0]
    else:
        base = to_slabs(mix_tokens([residual]))[:, 0]

    depth = tokens // tp // CHUNKS

    def cut(array, c):
        return array[:, c * depth : (c + 1) * depth]

    leaving = [cut(norm_back, c) for c in range(CHUNKS)]
    if by_permutes:
        leaving[1:] = [after(part, arrived[0]) for part in leaving[1:]]
    arrivals = [from_behind(part, "section", -1) for part in leaving]
    home = mix_features(after(norm_back, leaving[0]))
    blocks_of = []
    for c in range(CHUNKS):
        part = cut(base, c)
        arriving = arrivals[c]
        if c > 0:
            arriving = after(arriving, blocks[-1])
        grad_zero = arriving.astype(jnp.float32) + part.astype(jnp.float32)
        grad = jnp.where(upstream, grad_zero.astype(jnp.bfloat16), part)
        blocks = [over_rows(grad, turn) if turn else grad for turn in range(row)]
        blocks_of.append(blocks)
    attn_parts = []
    for c, blocks in enumerate(blocks_of):
        if c > 0:
            blocks[-1] = after(blocks[-1], attn_parts[-1][0])
        pieces = [half for block in blocks for half in (block, over_cores(block))]
        if c == 0:
            pieces[-1] = after(pieces[-1], home)
        terms = product(pieces, out_weight[0])
        first = lax.dynamic_index_in_dim(terms, (place - 1) % seq, 0, keepdims=False)
        attn_parts.append([first, terms])
    home = exchange(after(home, attn_parts[-1][0]), "tp")
    home = home.reshape(tokens, -1).astype(jnp.float32)
    own = (grad_one + home).astype(jnp.bfloat16)
    arrived = from_behind(own, "section", -1)
    input_zero = (arrived.astype(jnp.float32) + branch + home).astype(jnp.bfloat16)
    input_part = jnp.where(upstream, input_zero, own)
    for c, (mine, terms) in enumerate(attn_parts):
        for step in range(2, seq + 1):
            total = lax.ppermute(mine, "seq", [(q, (q + 1) % seq) for q in range(seq)])
            if c == 0 and step == 3:
                total = after(total, own)
            if c == CHUNKS - 1 and step == seq:
                total = after(total, input_part)
            mine = lax.dynamic_index_in_dim(terms, (place - step) % seq, 0, keepdims=False)
            mine = mine.astype(jnp.float32) + total.astype(jnp.float32)
            mine = mine.astype(jnp.bfloat16)
        attn_parts[c] = mine
    attn_part = jnp.concatenate(attn_parts, axis=1)
    order = []
    for t in range(tp):
        which = (here - t // CORES) % row * CORES + (lane + t) % CORES
        order.append(lax.dynamic_index_in_dim(attn_part, which, 0, keepdims=False))
    attn_part = jnp.concatenate(order, axis=0)

    return (attn_part[None], input_part[None])


def solution(mesh):
    in_specs = (
        P("section", "seq", "tp"),
        P("section", "tp"),
        P("section", "seq", "tp"),
        P("section", "tp", "seq"),
        P("section", "seq", "tp"),
        P("seq", "tp"),
        P("section", "tp", "seq"),
    )
    out_specs = (P("section", "seq", "tp"), P("section", "seq", "tp"))
    return jax.shard_map(body, mesh=mesh, in_specs=in_specs, out_specs=out_specs, check_vma=False)
```

```python
import jax
import jax.numpy as jnp
from jax import lax
from jax.experimental import pallas as pl
from jax.experimental.pallas import tpu as pltpu
from jax.sharding import PartitionSpec as P

D = 8192


epsilon = 1e-05
CORES = 2
CHUNKS = 2


def from_behind(block, axis, distance):
    devices = range(lax.axis_size(axis))
    route = [(i - distance, i) for i in devices if i - distance in devices]
    return lax.ppermute(block, axis, route)


def after(value, *others):
    return lax.optimization_barrier((value, *others))[0]


def sizes():
    seq, tp = lax.axis_size("seq"), lax.axis_size("tp")
    assert seq % tp == 0 and tp % CORES == 0
    return seq, tp, seq // tp


def over_rows(block, turn):
    tp = lax.axis_size("tp")
    return lax.ppermute(block, "tp", [(t, (t + turn * CORES) % tp) for t in range(tp)])


def over_cores(block):
    tp = lax.axis_size("tp")
    return lax.ppermute(block, "tp", [(t, t ^ 1) for t in range(tp)])


def exchange(block, axis):
    return lax.all_to_all(block, axis, 0, 0)


def mix_tokens(blocks):
    tp = lax.axis_size("tp")
    tokens, width = blocks[0].shape
    stacked = jnp.stack([block.reshape(tp, tokens // tp, width) for block in blocks], axis=1)
    return exchange(stacked, "tp")


def to_slabs(parts):
    seq, tp, ratio = sizes()
    _, count, tokens, width = parts.shape
    if ratio > 1:
        parts = parts.reshape(tp, count, tokens, ratio, width // ratio).transpose(0, 3, 1, 2, 4)
    return exchange(parts.reshape(seq, count, tokens, width // ratio), "seq")


def slabs_by_permutes(blocks):
    seq, tp, _ = sizes()
    place, lane = lax.axis_index("seq"), lax.axis_index("tp")
    here, core = lane // CORES, lane % CORES
    tokens, width = blocks[0].shape
    stacked = jnp.stack(
        [block.reshape(tp // CORES, CORES, tokens // tp, width) for block in blocks], axis=2
    )
    near = lax.dynamic_index_in_dim(stacked, here, 0, keepdims=False)
    far = over_rows(lax.dynamic_index_in_dim(stacked, 1 - here, 0, keepdims=False), 1)
    return near, far


def spread(near, far):
    seq, tp, _ = sizes()
    place, lane = lax.axis_index("seq"), lax.axis_index("tp")
    here, core = lane // CORES, lane % CORES
    arrived = []
    for j in range(seq):
        slot = place ^ j
        piece = jnp.where(
            slot // CORES == here,
            lax.dynamic_index_in_dim(near, slot % CORES, 0, keepdims=False),
            lax.dynamic_index_in_dim(far, slot % CORES, 0, keepdims=False),
        )
        route = []
        for q in range(seq):
            for t in range(tp):
                to = (t % CORES + (q ^ j) // CORES * CORES, t // CORES * CORES + (q ^ j) % CORES)
                if to != (q, t):
                    route.append((q * tp + t, to[0] * tp + to[1]))
        moved = lax.ppermute(piece, ("seq", "tp"), route)
        if j == 0:
            moved = jnp.where(core == place % CORES, piece, moved)
        arrived.append(moved)
    return arrived, place // CORES * CORES + core


def collect(arrived, slot):
    return jnp.stack([lax.select_n(slot ^ q, *arrived) for q in range(len(arrived))], axis=0)


def mix_features(block):
    seq, tp, ratio = sizes()
    _, tokens, width = block.shape
    parts = exchange(block, "seq")
    if ratio > 1:
        parts = parts.reshape(tp, ratio, tokens, width).transpose(0, 2, 1, 3)
    return parts.reshape(tp, tokens, width * ratio)


def gain_slab(gain):
    seq, tp, ratio = sizes()
    place, lane = lax.axis_index("seq"), lax.axis_index("tp")
    width = gain.shape[1] // ratio
    own = lax.dynamic_slice_in_dim(gain, place % ratio * width, width, 1)
    route = []
    for q in range(seq):
        for t in range(tp):
            to = (t * ratio + q % ratio, q // ratio)
            if to != (q, t):
                route.append((q * tp + t, to[0] * tp + to[1]))
    moved = lax.ppermute(own, ("seq", "tp"), route)
    stays = (place == lane * ratio + place % ratio) & (lane == place // ratio)
    return jnp.where(stays, own, moved)


def gather_seq(block):
    seq = lax.axis_size("seq")
    place = lax.axis_index("seq")
    arrived = [block]
    for turn in range(1, seq):
        route = [(q, (q + turn) % seq) for q in range(seq)]
        arrived.append(lax.ppermute(block, "seq", route))
    return jnp.stack([lax.select_n((place - q) % seq, *arrived) for q in range(seq)], axis=0)


def local_sums(values, gain, kv_share):
    return jnp.stack([jnp.sum(values * values, axis=-1), jnp.sum(gain * kv_share * values, axis=-1)])


def norm_backward(values, gain, kv_share, sums):
    short = lax.axis_size("seq") <= 2 * CORES
    squares, intersection = jnp.sum(gather_seq(sums), axis=0) if short else lax.psum(sums, "seq")
    inv_rms = lax.rsqrt(squares / D + epsilon)[..., None]
    return (
        inv_rms * gain * kv_share
        - values * (inv_rms * inv_rms * inv_rms) * intersection[..., None] / D
    )


def product_kernel(rows, weight, out):
    n, seq, depth, width = rows.shape
    terms = lax.dot_general(
        rows[...].reshape(-1, width),
        weight[...],
        (((1,), (1,)), ((), ())),
        preferred_element_type=jnp.float32,
    ).astype(out.dtype)
    for i in range(n):
        for q in range(seq):
            start = (i * seq + q) * depth
            out[q, i] = terms[start : start + depth]


def product(pieces, weight):
    rows = jnp.stack(pieces, axis=0)
    n, seq, depth, width = rows.shape
    heads = weight.shape[0]
    block = min(512, heads)
    return pl.pallas_call(
        product_kernel,
        out_shape=jax.ShapeDtypeStruct((seq, n, depth, heads), jnp.bfloat16),
        grid=(heads // block,),
        in_specs=[
            pl.BlockSpec((n, seq, depth, width), lambda i: (0, 0, 0, 0)),
            pl.BlockSpec((block, width), lambda i: (i, 0)),
        ],
        out_specs=pl.BlockSpec((seq, n, depth, block), lambda i: (0, 0, 0, i)),
        cost_estimate=pl.CostEstimate(
            flops=2 * n * seq * depth * width * heads,
            bytes_accessed=2 * heads * width + 2 * n * seq * depth * heads,
            transcendentals=0,
        ),
        compiler_params=pltpu.CompilerParams(
            dimension_semantics=("arbitrary",), vmem_limit_bytes=44 * 1024 * 1024
        ),
    )(rows, weight)


def body(layer_input, norm_gain, kv_cotangent, kv_weight, mlp_grads, output_cotangent, out_weight):
    seq, tp, ratio = sizes()
    row = tp // CORES
    upstream = lax.axis_index("section") == 0
    place, lane = lax.axis_index("seq"), lax.axis_index("tp")
    here, core = lane // CORES, lane % CORES
    tokens = kv_cotangent.shape[1]

    mixed = kv_cotangent[0].reshape(row, CORES, tokens // tp, -1)
    kept = lax.dynamic_index_in_dim(mixed, core, 1, keepdims=False)
    given = lax.dynamic_index_in_dim(mixed, 1 - core, 1, keepdims=False)
    given = over_cores(given)
    cotangent = jnp.concatenate([kept, given], axis=2)
    mlp = after(mlp_grads[0], cotangent)
    cotangent = gather_seq(cotangent)
    weights = jnp.concatenate([kv_weight[0], over_cores(kv_weight[0])], axis=0)

    branch = mlp_grads[0].astype(jnp.float32)
    grad_one = output_cotangent.astype(jnp.float32) + branch
    behind = from_behind(mlp, "section", -1)
    by_permutes = seq == tp == 2 * CORES
    gain = gain_slab(norm_gain)
    width = gain.shape[1]

    def kv_of(turn):
        part = lax.dynamic_index_in_dim(cotangent, (here + turn) % row, 1, keepdims=False)
        terms = jnp.dot(
            part.reshape(-1, part.shape[-1]), weights, preferred_element_type=jnp.float32
        )
        return terms.reshape(seq, tokens // tp, width)

    given = [kv_of(turn).astype(jnp.bfloat16) for turn in range(1, row)]
    residual = jnp.where(upstream, grad_one + after(behind, *given).astype(jnp.float32), grad_one)
    residual = after(residual.astype(jnp.bfloat16), *given)
    if by_permutes:
        near, far = slabs_by_permutes([layer_input[0]])
        values = collect(*spread(near, after(far, *given)))[:, 0]
    else:
        values = to_slabs(mix_tokens([layer_input[0]]))[:, 0]
    given = [over_rows(terms, turn) for turn, terms in enumerate(given, 1)]
    kv_share, values = lax.optimization_barrier((kv_of(0), values))
    for terms in given:
        kv_share = kv_share + terms.astype(jnp.float32)
    values = values.astype(jnp.float32)
    sums = local_sums(values, gain, kv_share)
    if by_permutes:
        near, far = slabs_by_permutes([residual])
        arrived, slot = spread(near, after(far, sums))
    norm_back = norm_backward(values, gain, kv_share, sums).astype(jnp.bfloat16)
    if by_permutes:
        base = collect(arrived, after(slot, norm_back))[:, 0]
    else:
        base = to_slabs(mix_tokens([residual]))[:, 0]

    depth = tokens // tp // CHUNKS

    def cut(array, c):
        return array[:, c * depth : (c + 1) * depth]

    leaving = [cut(norm_back, c) for c in range(CHUNKS)]
    if by_permutes:
        leaving[1:] = [after(part, arrived[0]) for part in leaving[1:]]
    arrivals = [from_behind(part, "section", -1) for part in leaving]
    home = mix_features(after(norm_back, leaving[0]))
    blocks_of = []
    for c in range(CHUNKS):
        part = cut(base, c)
        arriving = arrivals[c]
        if c > 0:
            arriving = after(arriving, blocks[-1])
        grad_zero = arriving.astype(jnp.float32) + part.astype(jnp.float32)
        grad = jnp.where(upstream, grad_zero.astype(jnp.bfloat16), part)
        blocks = [over_rows(grad, turn) if turn else grad for turn in range(row)]
        blocks_of.append(blocks)
    attn_parts = []
    for c, blocks in enumerate(blocks_of):
        if c > 0:
            blocks[-1] = after(blocks[-1], attn_parts[-1][0])
        pieces = [half for block in blocks for half in (block, over_cores(block))]
        terms = product(pieces, out_weight[0])
        first = lax.dynamic_index_in_dim(terms, (place - 1) % seq, 0, keepdims=False)
        if c == 0:
            first = after(first, home)
        attn_parts.append([first, terms])
    for c, (mine, terms) in enumerate(attn_parts):
        for step in range(2, seq + 1):
            total = lax.ppermute(mine, "seq", [(q, (q + 1) % seq) for q in range(seq)])
            if c == 0 and step == 2:
                total = after(total, attn_parts[-1][0])
            if c == 0 and step == 3:
                total = after(total, own)
            if c == CHUNKS - 1 and step == seq:
                total = after(total, input_part)
            mine = lax.dynamic_index_in_dim(terms, (place - step) % seq, 0, keepdims=False)
            mine = mine.astype(jnp.float32) + total.astype(jnp.float32)
            mine = mine.astype(jnp.bfloat16)
            if c == 0 and step == 2:
                home = exchange(after(home, mine), "tp")
                home = home.reshape(tokens, -1).astype(jnp.float32)
                own = (grad_one + home).astype(jnp.bfloat16)
                arrived = from_behind(own, "section", -1)
                input_zero = (arrived.astype(jnp.float32) + branch + home).astype(jnp.bfloat16)
                input_part = jnp.where(upstream, input_zero, own)
        attn_parts[c] = mine
    attn_part = jnp.concatenate(attn_parts, axis=1)
    order = []
    for t in range(tp):
        which = (here - t // CORES) % row * CORES + (lane + t) % CORES
        order.append(lax.dynamic_index_in_dim(attn_part, which, 0, keepdims=False))
    attn_part = jnp.concatenate(order, axis=0)

    return (attn_part[None], input_part[None])


def solution(mesh):
    in_specs = (
        P("section", "seq", "tp"),
        P("section", "tp"),
        P("section", "seq", "tp"),
        P("section", "tp", "seq"),
        P("section", "seq", "tp"),
        P("seq", "tp"),
        P("section", "tp", "seq"),
    )
    out_specs = (P("section", "seq", "tp"), P("section", "seq", "tp"))
    return jax.shard_map(body, mesh=mesh, in_specs=in_specs, out_specs=out_specs, check_vma=False)
```
